512 devices in a mesh: bulk: 32 (over z, y_hi), blk: 16 (over y_lo, x, core).
Axes of the slice: x: 4, y: 8 (y_hi: 4, y_lo: 2; y = y_hi * 2 + y_lo), z: 8, core: 2. Of those that a mesh axis runs over, the one named last changes fastest.
Arguments:
- aux_factors: bfloat16 [64, 1024, 4096], P('bulk', None, 'blk')
- tile_cols: int32 [16, 9], P('blk'), may hold values from -1 to 15, as said below
Outputs:
- exchange_tiles: float32 [144, 256, 256], P('blk', 'bulk')
The draws below stay inside these ranges and needn't reach their ends.
Inputs may be any that keep to these rules, and one draw needn't show every extreme that they name: `tile_cols`: row a lists distinct blocks, a itself first; every unordered pair of blocks stands in exactly one of its two rows; -1 marks empty slots, which come last; some row has no empty slot.
All inputs are finite; a program needn't handle non-finite values.
Results may differ from the reference program's by a relative error of at most 0.0003.
Values may be sent and summed in bfloat16 or wider, within the bound.
No kernel may reach another device: no remote copies, remote signals or barrier semaphores. Data moves between devices by JAX's collectives and lax.ppermute only.
A program may use at most 64 MiB of HBM per device.

```python
import jax
import jax.numpy as jnp

BLK_DEV = 256
NOCC = 1024
AUX = 64
NBLOCKS = 16
NBF = 4096
SLOTS = 9


def draw_aux_factors(key, part):
    key = jax.random.fold_in(key, 11)
    scale = float(AUX * NOCC) ** (-0.25)
    values = jax.random.normal(key, (AUX, NOCC, NBF), jnp.float32)
    return (values * scale).astype(jnp.bfloat16)


def draw_tile_cols(key, part):
    key = jax.random.fold_in(key, 23)
    order = jax.random.permutation(key, NBLOCKS).astype(jnp.int32)
    ranks = jnp.argsort(order, stable=True).astype(jnp.int32)
    offsets = jnp.arange(SLOTS, dtype=jnp.int32)
    places = (ranks[:, None] + offsets[None, :]) % NBLOCKS
    columns = order[places]
    keep = (offsets[None, :] < SLOTS - 1) | (ranks[:, None] < NBLOCKS // 2)
    return jnp.where(keep, columns, -1).astype(jnp.int32)


def setup_inputs(seed: int = 0) -> dict:
    keys = jax.random.split(jax.random.key(seed), 3)
    aux_factors = draw_aux_factors(jax.random.fold_in(keys[2], 71), 0)
    tile_cols = draw_tile_cols(jax.random.fold_in(keys[2], 71), 0)
    return {"aux_factors": aux_factors, "tile_cols": tile_cols}


def reference(aux_factors, tile_cols):
    flat = aux_factors.reshape(AUX * NOCC, NBF)
    whole = jnp.dot(flat.T, flat, preferred_element_type=jnp.float32)
    blocked = whole.reshape(NBLOCKS, BLK_DEV, NBLOCKS, BLK_DEV).transpose(0, 2, 1, 3)
    rows_index = jnp.arange(NBLOCKS, dtype=jnp.int32)[:, None]
    safe_cols = jnp.maximum(tile_cols, 0).astype(jnp.int32)
    tiles = blocked[rows_index, safe_cols]
    valid = (tile_cols >= 0)[:, :, None, None]
    tiles = jnp.where(valid, tiles, jnp.zeros_like(tiles))
    return tiles.reshape(NBLOCKS * SLOTS, BLK_DEV, BLK_DEV)
```

```python
import functools

import jax
import jax.numpy as jnp
import numpy as np
from jax import lax
from jax.experimental import pallas as pl
from jax.experimental.pallas import tpu as pltpu
from jax.sharding import Mesh
from jax.sharding import PartitionSpec as P

Z, H, L, X, C = 8, 4, 2, 4, 2
BLK = ("l", "x", "c")
BULK = ("z", "h")
SLOTS = 9
W = 256
ROWS = 1024


def place(l, x, c):
    return ((l % L) * X + x % X) * C + c % C


def far(x):
    return (x % X) // 2


def sib_of(l, x, c):
    return (l, x, 1 - c)


def x_of(l, x, c):
    return (l, (x + 1) % X, c)


def w_of(l, x, c):
    return (l, (x - 1) % X, c ^ l ^ far(x))


def v_of(l, x, c):
    return (1 - l, (x + 1) % X, c ^ l)


def v_via(l, x, c):
    return (1 - l, x, c ^ l)


ALL = [(l, x, c) for l in range(L) for x in range(X) for c in range(C)]


def fetch(value, role):
    return lax.ppermute(value, BLK, [(place(*role(*d)), place(*d)) for d in ALL])


def hand(value, role):
    return lax.ppermute(value, BLK, [(place(*d), place(*role(*d))) for d in ALL])


def table(f):
    return np.array([f(*d) for d in ALL], np.int32)


def candidates(l, x, c):
    me = (l, x, c)
    inverse = {}
    for d in ALL:
        for name, role in (("x", x_of), ("w", w_of), ("v", v_of)):
            if role(*d) == me:
                inverse[name] = d
    out = [place(*me), place(*sib_of(*me)), place(*x_of(*me)), place(*v_of(*me))]
    s = sib_of(*me)
    out += [place(*x_of(*s)), place(*v_of(*s))]
    h = inverse["x"]
    out += [place(*h), place(*sib_of(*h)), place(*w_of(*h)), place(*v_of(*h))]
    h = inverse["v"]
    out += [place(*x_of(*h)), place(*h), place(*sib_of(*h)), place(*w_of(*h))]
    h = inverse["w"]
    out += [place(*x_of(*h)), place(*v_of(*h))]
    assert sorted(out) == list(range(16)), out
    return out


def tiles_kernel(plan, n_in, first, keep_ref, *refs):
    ins, out_ref = refs[:n_in], refs[-1]
    step = pl.program_id(0)

    def dot(a, b):
        return lax.dot_general(
            a, b, (((0,), (0,)), ((), ())), preferred_element_type=jnp.float32
        )

    for i, (lhs, rhs, flag) in enumerate(plan):

        @pl.when(step == i)
        def _(lhs=lhs, rhs=rhs, flag=flag):
            tile = dot(ins[lhs[0]][...], ins[rhs[0]][...])
            tile += dot(ins[lhs[1]][...], ins[rhs[1]][...])
            if flag is None:
                out_ref[...] = tile.reshape(out_ref.shape)
            else:

                @pl.when(keep_ref[flag] != 0)
                def _():
                    out_ref[...] = tile.reshape(out_ref.shape)

                @pl.when(keep_ref[flag] == 0)
                def _():
                    out_ref[...] = tile.T.reshape(out_ref.shape)


def tiles(plan, first, keep, ins, out=None):
    shape = (Z, H, SLOTS, W // (Z * H), W)
    n = len(ins)
    in_specs = [pl.BlockSpec(memory_space=pltpu.SMEM)]
    in_specs += [pl.BlockSpec((ROWS, W), lambda i: (0, 0)) for _ in ins]
    args = [keep, *ins]
    aliases = {}
    if out is not None:
        in_specs.append(pl.BlockSpec(memory_space=pl.ANY))
        aliases = {len(args): 0}
        args.append(out)
    return pl.pallas_call(
        functools.partial(tiles_kernel, plan, n, first),
        grid=(len(plan),),
        out_shape=jax.ShapeDtypeStruct(shape, jnp.float32),
        in_specs=in_specs,
        out_specs=pl.BlockSpec(
            (Z, H, 1, W // (Z * H), W), lambda i: (0, 0, first + i, 0, 0)
        ),
        input_output_aliases=aliases,
        compiler_params=pltpu.CompilerParams(vmem_limit_bytes=40 * 2**20),
        cost_estimate=pl.CostEstimate(
            flops=len(plan) * 4 * W * W * ROWS,
            bytes_accessed=n * ROWS * W * 2 + len(plan) * W * W * 4,
            transcendentals=0,
        ),
    )(*args)


def local(aux_factors, tile_cols):
    row = tile_cols
    a1, a2 = aux_factors[0], aux_factors[1]
    me = lax.axis_index(BLK)

    x1 = fetch(a1, x_of)
    w1 = fetch(a1, w_of)
    b1 = fetch(a1, sib_of)
    x2 = fetch(a2, x_of)
    w2 = fetch(a2, w_of)
    b2 = fetch(a2, sib_of)
    row_x = fetch(row, x_of)[0]
    row_v = fetch(row, v_of)[0]
    v1 = fetch(x1, v_via)
    v2 = fetch(x2, v_via)

    ids = [
        jnp.asarray(table(lambda *d, r=r: place(*r(*d))))[me]
        for r in (sib_of, w_of, v_of)
    ]
    id_b, id_w, id_v = ids
    keep = jnp.stack(
        [
            jnp.any(row_x == me),
            jnp.any(row_x == id_b),
            jnp.any(row_x == id_w),
            jnp.any(row_x == id_v),
            jnp.any(row_v == me),
            jnp.any(row_v == id_b),
            jnp.any(row_v == id_w),
        ]
    ).astype(jnp.int32)

    a, b, x, w, v = (0, 1), (2, 3), (4, 5), (6, 7), (8, 9)
    early = [a1, a2, b1, b2, x1, x2, w1, w2]
    parts = tiles(
        [(a, a, None), (a, b, None), (x, a, 0), (x, b, 1), (x, w, 2)], 0, keep, early
    )
    parts = tiles(
        [(x, v, 3), (v, a, 4), (v, b, 5), (v, w, 6)],
        5,
        keep,
        early + [v1, v2],
        parts,
    )

    part = lax.psum_scatter(
        parts.reshape(Z, H * SLOTS * 8, W), "z", scatter_dimension=0, tiled=True
    )
    part = part.reshape(H, SLOTS, 8, W)
    part = lax.all_to_all(part, "h", 0, 0, tiled=True)
    done = part.sum(0)

    to_sib = hand(jnp.stack([done[3], done[7]]), sib_of)
    to_x = hand(done[2:6], x_of)
    to_v = hand(done[5:9], v_of)
    to_w = hand(jnp.stack([done[4], done[8]]), w_of)
    slabs = [done[0], done[1], done[2], done[6]]
    slabs += [to_sib[0], to_sib[1]]
    slabs += [to_x[i] for i in range(4)]
    slabs += [to_v[i] for i in range(4)]
    slabs += [to_w[0], to_w[1]]
    others = jnp.asarray(table(candidates))[me]
    wanted = row[0][:, None] == others[None, :]
    out = jnp.zeros((SLOTS, 8, W), jnp.float32)
    for k, slab in enumerate(slabs):
        out = out + jnp.where(wanted[:, k][:, None, None], slab[None], 0.0)
    return out


def solution(mesh):
    fine = Mesh(mesh.devices.reshape(Z, H, L, X, C), (*BULK, *BLK))
    in_specs = (P(BULK, None, BLK), P(BLK, None))
    out_specs = P(BLK, BULK, None)
    return jax.shard_map(
        local, mesh=fine, in_specs=in_specs, out_specs=out_specs, check_vma=False
    )
```

```python
import functools

import jax
import jax.numpy as jnp
import numpy as np
from jax import lax
from jax.experimental import pallas as pl
from jax.experimental.pallas import tpu as pltpu
from jax.sharding import Mesh
from jax.sharding import PartitionSpec as P

Z, H, L, X, C = 8, 4, 2, 4, 2
BLK = ("l", "x", "c")
BULK = ("z", "h")
SLOTS = 9
W = 256
ROWS = 1024
EARLY, LATE = 5, 4
SLAB = W // (Z * H)


def place(l, x, c):
    return (l * X + x) * C + c


def far(x):
    return x // 2


def sib_of(l, x, c):
    return (l, x, 1 - c)


def x_of(l, x, c):
    return (l, (x + 1) % X, c)


def w_of(l, x, c):
    return (l, (x + X - 1) % X, c ^ l ^ far(x))


def v_of(l, x, c):
    return (1 - l, (x + 1) % X, c ^ l)


def v_via(l, x, c):
    return (1 - l, x, c ^ l)


ALL = [(l, x, c) for l in range(L) for x in range(X) for c in range(C)]


def fetch(value, role):
    return lax.ppermute(value, BLK, [(place(*role(*d)), place(*d)) for d in ALL])


def hand(value, role):
    return lax.ppermute(value, BLK, [(place(*d), place(*role(*d))) for d in ALL])


def candidates(l, x, c):
    me = (l, x, c)
    inverse = {}
    for d in ALL:
        for name, role in (("x", x_of), ("w", w_of), ("v", v_of)):
            if role(*d) == me:
                inverse[name] = d
    out = [place(*me), place(*sib_of(*me)), place(*x_of(*me)), place(*v_of(*me))]
    s = sib_of(*me)
    out += [place(*x_of(*s)), place(*v_of(*s))]
    h = inverse["x"]
    out += [place(*h), place(*sib_of(*h)), place(*w_of(*h)), place(*v_of(*h))]
    h = inverse["v"]
    out += [place(*x_of(*h)), place(*h), place(*sib_of(*h)), place(*w_of(*h))]
    h = inverse["w"]
    out += [place(*x_of(*h)), place(*v_of(*h))]
    assert sorted(out) == list(range(16)), out
    return out


def position():
    return tuple(lax.axis_index(name) for name in BLK)


def dot(a, b):
    return lax.dot_general(
        a, b, (((0,), (0,)), ((), ())), preferred_element_type=jnp.float32
    )


def product(lhs, rhs):
    return dot(lhs[0], rhs[0]) + dot(lhs[1], rhs[1])


def owns(carrier, block):
    row = carrier[ROWS:].astype(jnp.float32)
    return jnp.max(jnp.where(row == block.astype(jnp.float32), 1.0, 0.0)) > 0.5


def early_kernel(a, b, x1, x2, w, out):
    me = position()
    x = (x1[:ROWS], x2[...])

    def put(slot, tile):
        out[:, :, slot] = tile.reshape(Z, H, SLAB, W)

    def settle(slot, rhs, block):
        tile = product(x, rhs)
        kept = owns(x1, place(*block))

        @pl.when(kept)
        def _():
            put(slot, tile)

        @pl.when(jnp.logical_not(kept))
        def _():
            put(slot, tile.T)

    put(0, product(a, a))
    put(1, product(a, b))
    settle(2, a, me)
    settle(3, b, sib_of(*me))
    settle(4, w, w_of(*me))


def late_kernel(a, b, x1, x2, w, v1, v2, out):
    me = position()
    x, v = (x1[:ROWS], x2[...]), (v1[:ROWS], v2[...])

    def put(slot, tile):
        tile = tile.reshape(Z, H, SLAB, W)
        for h in range(H):
            out[h, :, slot] = tile[:, h]

    def settle(slot, rhs, block):
        tile = product(v, rhs)
        kept = owns(v1, place(*block))

        @pl.when(kept)
        def _():
            put(slot, tile)

        @pl.when(jnp.logical_not(kept))
        def _():
            put(slot, tile.T)

    settle(0, x, x_of(*me))
    settle(1, a, me)
    settle(2, b, sib_of(*me))
    settle(3, w, w_of(*me))


def call(kernel, shape, n_tiles, *ins):
    vmem = pl.BlockSpec(memory_space=pltpu.VMEM)
    return pl.pallas_call(
        kernel,
        out_shape=jax.ShapeDtypeStruct(shape, jnp.float32),
        in_specs=[vmem] * len(ins),
        out_specs=vmem,
        compiler_params=pltpu.CompilerParams(vmem_limit_bytes=40 * 2**20),
        cost_estimate=pl.CostEstimate(
            flops=n_tiles * 4 * W * W * ROWS,
            bytes_accessed=sum(v.size * 2 for v in ins) + n_tiles * W * W * 4,
            transcendentals=0,
        ),
    )(*ins)


def local(aux_factors, tile_cols):
    a = aux_factors
    row = jnp.pad(tile_cols.astype(jnp.bfloat16), ((0, 15), (0, W - SLOTS)), constant_values=-2)

    x1 = fetch(jnp.concatenate([a[0], row]), x_of)
    w = fetch(a, w_of)
    x2 = fetch(a[1], x_of)
    b = fetch(a, sib_of)
    v1 = fetch(x1, v_via)
    v2 = fetch(x2, v_via)

    early = call(early_kernel, (Z, H, EARLY, SLAB, W), EARLY, a, b, x1, x2, w)
    late = call(late_kernel, (H, Z, LATE, SLAB, W), LATE, a, b, x1, x2, w, v1, v2)

    early = lax.psum_scatter(
        early.reshape(Z, H * EARLY * SLAB, W), "z", scatter_dimension=0, tiled=True
    )
    late = late.reshape(H, Z * LATE * SLAB, W)
    late = lax.all_to_all(late, "h", 0, 0, tiled=True).sum(0)
    late = late.reshape(Z, LATE * SLAB, W)
    late = lax.all_to_all(late, "z", 0, 0, tiled=True).sum(0)
    early = early.reshape(H, EARLY * SLAB, W)
    early = lax.all_to_all(early, "h", 0, 0, tiled=True).sum(0)
    e = early.reshape(EARLY, SLAB, W)
    v = late.reshape(LATE, SLAB, W)

    to_sib = hand(jnp.stack([e[3], v[2]]), sib_of)
    to_x = hand(jnp.concatenate([e[2:5], v[0:1]]), x_of)
    to_v = hand(v, v_of)
    to_w = hand(jnp.stack([e[4], v[3]]), w_of)
    slabs = [e[0], e[1], e[2], v[1]]
    slabs += [to_sib[i] for i in range(2)]
    slabs += [to_x[i] for i in range(4)]
    slabs += [to_v[i] for i in range(4)]
    slabs += [to_w[i] for i in range(2)]
    me = lax.axis_index(BLK)
    others = jnp.asarray(np.array([candidates(*d) for d in ALL], np.int32))[me]
    wanted = tile_cols[0][:, None] == others[None, :]
    out = jnp.zeros((SLOTS, SLAB, W), jnp.float32)
    for k, slab in enumerate(slabs):
        out = out + jnp.where(wanted[:, k][:, None, None], slab[None], 0.0)
    return out


def solution(mesh):
    fine = Mesh(mesh.devices.reshape(Z, H, L, X, C), (*BULK, *BLK))
    in_specs = (P(BULK, None, BLK), P(BLK, None))
    out_specs = P(BLK, BULK, None)
    return jax.shard_map(
        local, mesh=fine, in_specs=in_specs, out_specs=out_specs, check_vma=False
    )
```

```python
import jax
import jax.numpy as jnp
import numpy as np
from jax import lax
from jax.experimental import pallas as pl
from jax.experimental.pallas import tpu as pltpu
from jax.sharding import Mesh
from jax.sharding import PartitionSpec as P

Z, H, L, X, C = 8, 4, 2, 4, 2
BLK = ("l", "x", "c")
BULK = ("z", "h")
N_BLK, N_BULK = L * X * C, Z * H
SLOTS = 9
W = 256
K = 2048
SLAB = W // N_BULK
EARLY = 8
DEPTH = 4


def place(l, x, c):
    return (l * X + x) * C + c


def own(l, x, c):
    return (l, x, c)


def sib(l, x, c):
    return (l, x, 1 - c)


def right(l, x, c):
    return (l, (x + 1) & 3, c)


def left(l, x, c):
    return (l, (x + 3) & 3, c ^ (x >> 1))


def flip(x):
    return (x + 3) >> 2


def over(l, x, c):
    return (1 - l, x, c ^ flip(x))


def diag(l, x, c):
    return (1 - l, (x + 1) & 3, c ^ (x >> 1) ^ l)


def diag_via(l, x, c):
    return (l, (x + 1) & 3, c ^ (x >> 1) ^ l ^ flip((x + 1) & 3))


def mate_bit(l, x):
    return flip(x) ^ l


def mate(l, x, c):
    return (l, x, c ^ mate_bit(l, x))


ALL = [(l, x, c) for l in range(L) for x in range(X) for c in range(C)]
TILES = [
    (own, own),
    (own, sib),
    (right, own),
    (right, sib),
    (right, over),
    (right, left),
    (over, left),
    (over, mate),
    (left, diag),
]


def mailing(l, x, c):
    me = (l, x, c)
    out = {}
    for t, (p, q) in enumerate(TILES):
        p, q = p(*me), q(*me)
        ends = [(p, q)] if t < 2 else [(p, q), (q, p)]
        for owner, other in ends:
            out.setdefault(place(*owner), []).append((t, place(*other)))
    return out


def addresses():
    table = np.full((N_BLK, N_BLK), -1, np.int32)
    for d in ALL:
        for owner, items in mailing(*d).items():
            assert len(items) <= DEPTH
            for slot, (_, other) in enumerate(items):
                assert table[owner, other] < 0
                table[owner, other] = place(*d) * DEPTH + slot
    assert (table >= 0).all()
    return table


def stamps():
    rows = []
    for d in ALL:
        where = {}
        for owner, items in mailing(*d).items():
            for slot, (t, _) in enumerate(items):
                where[(t, owner)] = owner * DEPTH + slot
        row = []
        for t, (p, q) in enumerate(TILES):
            row.append(where[(t, place(*p(*d)))])
            if t >= 2:
                row.append(where[(t, place(*q(*d)))])
        rows.append(row)
    return np.array(rows, np.int32)


def fetch(value, role):
    return lax.ppermute(value, BLK, [(place(*role(*d)), place(*d)) for d in ALL])


def position():
    return tuple(lax.axis_index(name) for name in BLK)


def dot(a, b):
    return lax.dot_general(
        a, b, (((0,), (0,)), ((), ())), preferred_element_type=jnp.float32
    )


def owns(carrier, block):
    row = carrier[K:].astype(jnp.float32)
    return jnp.max(jnp.where(row == block.astype(jnp.float32), 1.0, 0.0)) > 0.5


def settle(carrier, rhs, block, put):
    tile = dot(carrier[:K], rhs)
    kept = owns(carrier, place(*block))

    @pl.when(kept)
    def _():
        put(tile)

    @pl.when(jnp.logical_not(kept))
    def _():
        put(tile.T)


def early_kernel(a, b, xr, xl, yo, out):
    me = position()

    def put(slot):
        def write(tile):
            out[:, pl.ds(slot * SLAB, SLAB)] = tile.reshape(N_BULK, SLAB, W)

        return write

    put(0)(dot(a[:K], a[:K]))
    put(1)(dot(a[:K], b[:K]))
    settle(xr, a[:K], own(*me), put(2))
    settle(xr, b[:K], sib(*me), put(3))
    settle(xr, yo[:K], over(*me), put(4))
    settle(xr, xl[:K], left(*me), put(5))
    settle(yo, xl[:K], left(*me), put(6))
    mine = mate_bit(*me[:2]) == 0

    @pl.when(mine)
    def _():
        settle(yo, a[:K], mate(*me), put(7))

    @pl.when(jnp.logical_not(mine))
    def _():
        settle(yo, b[:K], mate(*me), put(7))


def late_kernel(xl, vd, out):
    def put(tile):
        out[...] = tile.reshape(N_BULK, SLAB, W)

    settle(xl, vd[:K], diag(*position()), put)


def pack_kernel(stamp, e, v, out):
    me = place(*position())
    k = 0
    for t in range(SLOTS):
        tile = e[pl.ds(t * SLAB, SLAB)] if t < EARLY else v[...]
        for _ in range(1 if t < 2 else 2):
            out[stamp[me, k]] = tile
            k += 1


def pick_kernel(table, cols, got, out):
    me = place(*position())
    for j in range(SLOTS):
        b = cols[0, j]

        @pl.when(b >= 0)
        def _():
            out[j] = got[table[me, jnp.maximum(b, 0)]]

        @pl.when(b < 0)
        def _():
            out[j] = jnp.zeros((SLAB, W), jnp.float32)


def call(kernel, shape, n_smem, n_tiles, *ins):
    vmem = pl.BlockSpec(memory_space=pltpu.VMEM)
    smem = pl.BlockSpec(memory_space=pltpu.SMEM)
    return pl.pallas_call(
        kernel,
        out_shape=jax.ShapeDtypeStruct(shape, jnp.float32),
        in_specs=[smem] * n_smem + [vmem] * (len(ins) - n_smem),
        out_specs=vmem,
        compiler_params=pltpu.CompilerParams(vmem_limit_bytes=40 * 2**20),
        cost_estimate=pl.CostEstimate(
            flops=n_tiles * 2 * W * W * K,
            bytes_accessed=sum(v.size * v.dtype.itemsize for v in ins)
            + 4 * int(np.prod(shape)),
            transcendentals=0,
        ),
    )(*ins)


def exchange(parts):
    got = lax.all_to_all(parts, BULK, 0, 0, tiled=True)
    return got.sum(0)


def local(aux_factors, tile_cols):
    row = jnp.pad(
        tile_cols.astype(jnp.bfloat16),
        ((0, 15), (0, W - SLOTS)),
        constant_values=-2,
    )
    a = jnp.concatenate([aux_factors.reshape(K, W), row])
    yo = fetch(a, over)
    xr = fetch(a, right)
    xl = fetch(a, left)
    b = fetch(a, sib)
    vd = fetch(yo, diag_via)

    early = call(early_kernel, (N_BULK, EARLY * SLAB, W), 0, EARLY, a, b, xr, xl, yo)
    late = call(late_kernel, (N_BULK, SLAB, W), 0, 1, xl, vd)
    early, late = exchange(early), exchange(late)

    mail = call(
        pack_kernel, (N_BLK * DEPTH, SLAB, W), 1, 0, jnp.asarray(stamps()), early, late
    )
    mail = lax.all_to_all(mail, BLK, 0, 0, tiled=True)
    return call(
        pick_kernel,
        (SLOTS, SLAB, W),
        2,
        0,
        jnp.asarray(addresses()),
        tile_cols,
        mail,
    )


def solution(mesh):
    fine = Mesh(mesh.devices.reshape(Z, H, L, X, C), (*BULK, *BLK))
    in_specs = (P(BULK, None, BLK), P(BLK, None))
    out_specs = P(BLK, BULK, None)
    return jax.shard_map(
        local, mesh=fine, in_specs=in_specs, out_specs=out_specs, check_vma=False
    )
```

```python
import jax
import jax.numpy as jnp
import numpy as np
from jax import lax
from jax.experimental import pallas as pl
from jax.experimental.pallas import tpu as pltpu
from jax.sharding import Mesh
from jax.sharding import PartitionSpec as P

Z, H, L, X, C = 8, 4, 2, 4, 2
BLK = ("l", "x", "c")
BULK = ("z", "h")
N_BLK, N_BULK = L * X * C, Z * H
SLOTS = 9
W = 256
K = 2048
SLAB = W // N_BULK
EARLY = 8
DEPTH = 4
DATA, MARK, TOP = EARLY * W // Z, 16, 14.0


def place(l, x, c):
    return (l * X + x) * C + c


def own(l, x, c):
    return (l, x, c)


def sib(l, x, c):
    return (l, x, 1 - c)


def right(l, x, c):
    return (l, (x + 1) & 3, c)


def left(l, x, c):
    return (l, (x + 3) & 3, c ^ (x >> 1))


def flip(x):
    return (x + 3) >> 2


def over(l, x, c):
    return (1 - l, x, c ^ flip(x))


def diag(l, x, c):
    return (1 - l, (x + 1) & 3, c ^ (x >> 1) ^ l)


def diag_via(l, x, c):
    return (l, (x + 1) & 3, c ^ (x >> 1) ^ l ^ flip((x + 1) & 3))


def mate_bit(l, x):
    return flip(x) ^ l


def mate(l, x, c):
    return (l, x, c ^ mate_bit(l, x))


ALL = [(l, x, c) for l in range(L) for x in range(X) for c in range(C)]
TILES = [
    (own, own),
    (own, sib),
    (right, own),
    (right, sib),
    (right, over),
    (right, left),
    (over, left),
    (over, mate),
    (left, diag),
]


def mailing(l, x, c):
    me = (l, x, c)
    out = {}
    for t, (p, q) in enumerate(TILES):
        p, q = p(*me), q(*me)
        ends = [(p, q)] if t < 2 else [(p, q), (q, p)]
        for owner, other in ends:
            out.setdefault(place(*owner), []).append((t, place(*other)))
    return out


def addresses():
    table = np.full((N_BLK, N_BLK), -1, np.int32)
    for d in ALL:
        for owner, items in mailing(*d).items():
            assert len(items) <= DEPTH
            for slot, (_, other) in enumerate(items):
                assert table[owner, other] < 0
                table[owner, other] = place(*d) * DEPTH + slot
    assert (table >= 0).all()
    return table


def stamps():
    rows = []
    for d in ALL:
        where = {}
        for owner, items in mailing(*d).items():
            for slot, (t, _) in enumerate(items):
                where[(t, owner)] = owner * DEPTH + slot
        row = []
        for t, (p, q) in enumerate(TILES):
            row.append(where[(t, place(*p(*d)))])
            if t >= 2:
                row.append(where[(t, place(*q(*d)))])
        rows.append(row)
    return np.array(rows, np.int32)


def fetch(value, role):
    return lax.ppermute(value, BLK, [(place(*role(*d)), place(*d)) for d in ALL])


def position():
    return tuple(lax.axis_index(name) for name in BLK)


def dot(a, b):
    return lax.dot_general(
        a, b, (((0,), (0,)), ((), ())), preferred_element_type=jnp.float32
    )


def owns(carrier, block):
    row = carrier[K:].astype(jnp.float32)
    return jnp.max(jnp.where(row == block.astype(jnp.float32), 1.0, 0.0)) > 0.5


def settle(carrier, rhs, block, put):
    kept = owns(carrier, place(*block))

    @pl.when(kept)
    def _():
        put(dot(carrier[:K], rhs[:K]))

    @pl.when(jnp.logical_not(kept))
    def _():
        put(dot(rhs[:K], carrier[:K]))


def early_kernel(a, b, xr, xl, yo, out, scale):
    me = position()

    def put(slot):
        def write(tile):
            tile = tile.reshape(Z, H, SLAB, W)
            for h in range(H):
                row = (h * EARLY + slot) * SLAB
                out[:, pl.ds(row, SLAB)] = tile[:, h]

        return write

    put(0)(dot(a[:K], a[:K]))
    put(1)(dot(a[:K], b[:K]))
    settle(xr, a, own(*me), put(2))
    settle(xr, b, sib(*me), put(3))
    settle(xr, yo, over(*me), put(4))
    settle(xr, xl, left(*me), put(5))
    settle(yo, xl, left(*me), put(6))
    mine = mate_bit(*me[:2]) == 0

    @pl.when(mine)
    def _():
        settle(yo, a, mate(*me), put(7))

    @pl.when(jnp.logical_not(mine))
    def _():
        settle(yo, b, mate(*me), put(7))

    most = jnp.max(jnp.abs(out[0, :DATA]), axis=0, keepdims=True)
    for z in range(1, Z):
        peak = jnp.max(jnp.abs(out[z, :DATA]), axis=0, keepdims=True)
        most = jnp.maximum(most, peak)
    most = jnp.maximum(jnp.max(most, axis=1, keepdims=True), 1e-30)
    power = jnp.ceil(jnp.log2(jnp.broadcast_to(most, (8, 128))))
    spread = 1.0 + lax.axis_index("z").astype(jnp.float32) / Z
    by = jnp.exp2(TOP - power) * spread
    scale[...] = by
    mark = jnp.broadcast_to((power / by)[:1, :1], (MARK, W))
    for z in range(Z):
        out[z, DATA:] = mark


def late_kernel(xl, vd, out):
    def put(tile):
        out[...] = tile.reshape(Z, W // Z, W)

    settle(xl, vd, diag(*position()), put)


def pack_kernel(stamp, got, out):
    me = place(*position())
    k = 0
    for t in range(SLOTS):
        rows = pl.ds(t * SLAB, SLAB)
        tile = got[0, rows] + got[1, rows] + got[2, rows] + got[3, rows]
        for _ in range(1 if t < 2 else 2):
            out[stamp[me, k]] = tile
            k += 1


def pick_kernel(table, cols, got, out):
    me = place(*position())
    for j in range(SLOTS):
        b = cols[0, j]

        @pl.when(b >= 0)
        def _():
            out[j] = got[table[me, jnp.maximum(b, 0)]]

        @pl.when(b < 0)
        def _():
            out[j] = jnp.zeros((SLAB, W), jnp.float32)


def call(kernel, shapes, n_smem, n_tiles, *ins):
    vmem = pl.BlockSpec(memory_space=pltpu.VMEM)
    smem = pl.BlockSpec(memory_space=pltpu.SMEM)
    size = sum(int(np.prod(shape)) for shape in shapes)
    return pl.pallas_call(
        kernel,
        out_shape=[jax.ShapeDtypeStruct(shape, jnp.float32) for shape in shapes],
        in_specs=[smem] * n_smem + [vmem] * (len(ins) - n_smem),
        out_specs=[vmem] * len(shapes),
        compiler_params=pltpu.CompilerParams(vmem_limit_bytes=40 * 2**20),
        cost_estimate=pl.CostEstimate(
            flops=n_tiles * 2 * W * W * K,
            bytes_accessed=4 * size + sum(v.size * v.dtype.itemsize for v in ins),
            transcendentals=0,
        ),
    )(*ins)


def everywhere(value, axes):
    return lax.all_to_all(value, axes, 0, 0, tiled=True)


def local(aux_factors, tile_cols):
    row = jnp.pad(
        tile_cols.astype(jnp.bfloat16),
        ((0, 15), (0, W - SLOTS)),
        constant_values=-2,
    )
    a = jnp.concatenate([aux_factors.reshape(K, W), row])
    yo = fetch(a, over)
    xr = fetch(a, right)
    xl = fetch(a, left)
    b = fetch(a, sib)
    yo, xr, xl = lax.optimization_barrier((yo, xr, xl))
    vd = fetch(yo, diag_via)

    early, scale = call(
        early_kernel, [(Z, DATA + MARK, W), (8, 128)], 0, EARLY, a, b, xr, xl, yo
    )
    early = everywhere((early * scale[0, 0]).astype(jnp.float16), "z")
    (late,) = call(late_kernel, [(Z, W // Z, W)], 0, 1, xl, vd)
    early, late = lax.optimization_barrier((early, late))
    late = everywhere(late, "z").sum(0)

    power = early[:, DATA:DATA + 1, :1].astype(jnp.float32)
    spread = 1.0 + lax.broadcasted_iota(jnp.float32, (Z, 1, 1), 0) / Z
    early = early[:, :DATA].astype(jnp.float32) * (jnp.exp2(power - TOP) / spread)
    early = early.sum(0).reshape(H, EARLY * SLAB, W)
    late = late.reshape(H, SLAB, W)

    parts = everywhere(jnp.concatenate([early, late], 1), "h")
    (mail,) = call(
        pack_kernel, [(N_BLK * DEPTH, SLAB, W)], 1, 0, jnp.asarray(stamps()), parts
    )
    mail = everywhere(mail, BLK)
    table = jnp.asarray(addresses())
    return call(pick_kernel, [(SLOTS, SLAB, W)], 2, 0, table, tile_cols, mail)[0]


def solution(mesh):
    fine = Mesh(mesh.devices.reshape(Z, H, L, X, C), (*BULK, *BLK))
    in_specs = (P(BULK, None, BLK), P(BLK, None))
    out_specs = P(BLK, BULK, None)
    return jax.shard_map(
        local, mesh=fine, in_specs=in_specs, out_specs=out_specs, check_vma=False
    )
```

```python
import jax
import jax.numpy as jnp
import numpy as np
from jax import lax
from jax.experimental import pallas as pl
from jax.experimental.pallas import tpu as pltpu
from jax.sharding import Mesh
from jax.sharding import PartitionSpec as P

Z, H, L, X, C = 8, 4, 2, 4, 2
BLK = ("l", "x", "c")
N_BLK, N_BULK = L * X * C, Z * H
BULK = ("z", "h")
SLOTS = 9
W = 256
K = 2048
HALF = K // 2
SLAB = W // N_BULK
DEPTH = 4
MARK, TOP = 16, 14.0


def place(l, x, c):
    return (l * X + x) * C + c


def own(l, x, c):
    return (l, x, c)


def sib(l, x, c):
    return (l, x, 1 - c)


def right(l, x, c):
    return (l, (x + 1) & 3, c)


def left(l, x, c):
    return (l, (x + 3) & 3, c ^ l ^ (x >> 1))


def diag(l, x, c):
    return (1 - l, (x + 1) & 3, c ^ l)


def diag_via(l, x, c):
    return (1 - l, x, c ^ l)


ALL = [(l, x, c) for l in range(L) for x in range(X) for c in range(C)]
TILES = [
    (own, own),
    (own, sib),
    (right, own),
    (right, sib),
    (right, left),
    (diag, right),
    (diag, own),
    (diag, sib),
    (diag, left),
]
GROUPS = (5, 4)


def mailing(l, x, c):
    me = (l, x, c)
    out = {}
    for t, (p, q) in enumerate(TILES):
        p, q = p(*me), q(*me)
        ends = [(p, q)] if t < 2 else [(p, q), (q, p)]
        for owner, other in ends:
            out.setdefault(place(*owner), []).append((t, place(*other)))
    return out


def addresses():
    table = np.full((N_BLK, N_BLK), -1, np.int32)
    for d in ALL:
        for owner, items in mailing(*d).items():
            assert len(items) <= DEPTH
            for slot, (_, other) in enumerate(items):
                assert table[owner, other] < 0
                table[owner, other] = place(*d) * DEPTH + slot
    assert (table >= 0).all()
    return table


def stamps():
    rows = []
    for d in ALL:
        where = {}
        for owner, items in mailing(*d).items():
            for slot, (t, _) in enumerate(items):
                where[(t, owner)] = owner * DEPTH + slot
        row = []
        for t, (p, q) in enumerate(TILES):
            row.append(where[(t, place(*p(*d)))])
            if t >= 2:
                row.append(where[(t, place(*q(*d)))])
        rows.append(row)
    return np.array(rows, np.int32)


def fetch(value, role):
    return lax.ppermute(value, BLK, [(place(*role(*d)), place(*d)) for d in ALL])


def position():
    return tuple(lax.axis_index(name) for name in BLK)


def dot(a, b):
    return lax.dot_general(
        a, b, (((0,), (0,)), ((), ())), preferred_element_type=jnp.float32
    )


def product(p, q):
    return dot(p[0][:HALF], q[0][:HALF]) + dot(p[1][...], q[1][...])


def owns(carrier, block):
    row = carrier[0][HALF:].astype(jnp.float32)
    return jnp.max(jnp.where(row == block.astype(jnp.float32), 1.0, 0.0)) > 0.5


def writer(out, slot, count):
    def put(tile):
        tile = tile.reshape(Z, H, SLAB, W)
        for h in range(H):
            out[:, pl.ds((h * count + slot) * SLAB, SLAB)] = tile[:, h]

    return put


def settle(carrier, rhs, block, put):
    kept = owns(carrier, place(*block))

    @pl.when(kept)
    def _():
        put(product(carrier, rhs))

    @pl.when(jnp.logical_not(kept))
    def _():
        put(product(rhs, carrier))


def squeeze(out):
    data = out.shape[1] - MARK
    most = jnp.zeros((1, W), jnp.float32)
    for z in range(Z):
        peak = jnp.max(jnp.abs(out[z, :data]), axis=0, keepdims=True)
        most = jnp.maximum(most, peak)
    most = jnp.maximum(jnp.max(most, axis=1, keepdims=True), 1e-30)
    power = jnp.ceil(jnp.log2(jnp.broadcast_to(most, (SLAB, W))))
    spread = 1.0 + lax.axis_index("z").astype(jnp.float32) / Z
    by = (jnp.exp2(TOP - power) * spread)[:1]
    for z in range(Z):
        out[z, :data] = out[z, :data] * by
        out[z, data:] = jnp.broadcast_to(power[:1], (MARK, W))


def early_kernel(a, b, w, x1, x2, out):
    a, b, w = ((r.at[0], r.at[1]) for r in (a, b, w))
    me = position()
    x = (x1, x2)
    writer(out, 0, 5)(product(a, a))
    writer(out, 1, 5)(product(a, b))
    settle(x, a, own(*me), writer(out, 2, 5))
    settle(x, b, sib(*me), writer(out, 3, 5))
    settle(x, w, left(*me), writer(out, 4, 5))
    squeeze(out)


def late_kernel(a, b, w, x1, x2, v1, v2, out):
    a, b, w = ((r.at[0], r.at[1]) for r in (a, b, w))
    me = position()
    x, v = (x1, x2), (v1, v2)
    settle(v, x, right(*me), writer(out, 0, 4))
    settle(v, a, own(*me), writer(out, 1, 4))
    settle(v, b, sib(*me), writer(out, 2, 4))
    settle(v, w, left(*me), writer(out, 3, 4))
    squeeze(out)


def pack_kernel(stamp, got, out):
    me = place(*position())
    k = 0
    for t in range(SLOTS):
        rows = pl.ds(t * SLAB, SLAB)
        tile = got[0, rows] + got[1, rows] + got[2, rows] + got[3, rows]
        for _ in range(1 if t < 2 else 2):
            out[stamp[me, k]] = tile
            k += 1


def pick_kernel(table, cols, got, out):
    me = place(*position())
    for j in range(SLOTS):
        b = cols[0, j]

        @pl.when(b >= 0)
        def _():
            out[j] = got[table[me, jnp.maximum(b, 0)]]

        @pl.when(b < 0)
        def _():
            out[j] = jnp.zeros((SLAB, W), jnp.float32)


def call(kernel, shape, n_smem, n_tiles, *ins):
    vmem = pl.BlockSpec(memory_space=pltpu.VMEM)
    smem = pl.BlockSpec(memory_space=pltpu.SMEM)
    return pl.pallas_call(
        kernel,
        out_shape=jax.ShapeDtypeStruct(shape, jnp.float32),
        in_specs=[smem] * n_smem + [vmem] * (len(ins) - n_smem),
        out_specs=vmem,
        compiler_params=pltpu.CompilerParams(vmem_limit_bytes=40 * 2**20),
        cost_estimate=pl.CostEstimate(
            flops=n_tiles * 2 * W * W * K,
            bytes_accessed=4 * int(np.prod(shape))
            + sum(v.size * v.dtype.itemsize for v in ins),
            transcendentals=0,
        ),
    )(*ins)


def everywhere(value, axes):
    return lax.all_to_all(value, axes, 0, 0, tiled=True)


def tiles(kernel, count, *ins):
    shape = (Z, count * W // Z + MARK, W)
    return call(kernel, shape, 0, count, *ins).astype(jnp.float16)


def total(got):
    data = got.shape[1] - MARK
    power = got[:, data : data + 1, :1].astype(jnp.float32)
    spread = 1.0 + lax.broadcasted_iota(jnp.float32, (Z, 1, 1), 0) / Z
    got = got[:, :data].astype(jnp.float32) * (jnp.exp2(power - TOP) / spread)
    return got.sum(0).reshape(H, data // H, W)


def local(aux_factors, tile_cols):
    row = jnp.pad(
        tile_cols.astype(jnp.bfloat16),
        ((0, 15), (0, W - SLOTS)),
        constant_values=-2,
    )
    a1, a2, a = lax.optimization_barrier(
        (jnp.concatenate([aux_factors[0], row]), aux_factors[1], aux_factors)
    )
    x1 = fetch(a1, right)
    w = fetch(a, left)
    x2 = fetch(a2, right)
    b = fetch(a, sib)
    v1 = fetch(x1, diag_via)
    v2 = fetch(x2, diag_via)

    x1, v1 = lax.optimization_barrier((x1, v1))
    early = tiles(early_kernel, GROUPS[0], a, b, w, x1, x2)
    early = everywhere(early, "z")
    late = tiles(late_kernel, GROUPS[1], a, b, w, x1, x2, v1, v2)
    early, late = lax.optimization_barrier((early, late))
    late = everywhere(late, "z")

    parts = jnp.concatenate([total(early), total(late)], 1)
    parts = everywhere(parts, "h")
    mail = call(pack_kernel, (N_BLK * DEPTH, SLAB, W), 1, 0, jnp.asarray(stamps()), parts)
    mail = everywhere(mail, BLK)
    table = jnp.asarray(addresses())
    return call(pick_kernel, (SLOTS, SLAB, W), 2, 0, table, tile_cols, mail)


def solution(mesh):
    fine = Mesh(mesh.devices.reshape(Z, H, L, X, C), (*BULK, *BLK))
    in_specs = (P(BULK, None, BLK), P(BLK, None))
    out_specs = P(BLK, BULK, None)
    return jax.shard_map(
        local, mesh=fine, in_specs=in_specs, out_specs=out_specs, check_vma=False
    )
```

```python
import jax
import jax.numpy as jnp
import numpy as np
from jax import lax
from jax.experimental import pallas as pl
from jax.experimental.pallas import tpu as pltpu
from jax.sharding import Mesh
from jax.sharding import PartitionSpec as P

Z, H, L, X, C = 8, 4, 2, 4, 2
BLK = ("l", "x", "c")
N_BLK, N_BULK = L * X * C, Z * H
BULK = ("z", "h")
SLOTS = 9
W = 256
K = 2048
PARTS = (768, 768, 512)
STARTS = (0, 768, 1536)
SLAB = W // N_BULK
DEPTH = 4
TOP = 14.0


def place(l, x, c):
    return (l * X + x) * C + c


def own(l, x, c):
    return (l, x, c)


def sib(l, x, c):
    return (l, x, 1 - c)


def right(l, x, c):
    return (l, (x + 1) & 3, c)


def left(l, x, c):
    return (l, (x + 3) & 3, c ^ l ^ (x >> 1))


def diag(l, x, c):
    return (1 - l, (x + 1) & 3, c ^ l)


def diag_via(l, x, c):
    return (1 - l, x, c ^ l)


ALL = [(l, x, c) for l in range(L) for x in range(X) for c in range(C)]
TILES = [
    (own, own),
    (own, sib),
    (right, own),
    (right, sib),
    (right, left),
    (diag, right),
    (diag, own),
    (diag, sib),
    (diag, left),
]
EARLY, LATE = 5, 4


def mailing(l, x, c):
    me = (l, x, c)
    out = {}
    for t, (p, q) in enumerate(TILES):
        p, q = p(*me), q(*me)
        ends = [(p, q)] if t < 2 else [(p, q), (q, p)]
        for owner, other in ends:
            out.setdefault(place(*owner), []).append((t, place(*other)))
    return out


def addresses():
    table = np.full((N_BLK, N_BLK), -1, np.int32)
    for d in ALL:
        for owner, items in mailing(*d).items():
            assert len(items) <= DEPTH
            for slot, (_, other) in enumerate(items):
                assert table[owner, other] < 0
                table[owner, other] = place(*d) * DEPTH + slot
    assert (table >= 0).all()
    return table


def stamps():
    rows = []
    for d in ALL:
        where = {}
        for owner, items in mailing(*d).items():
            for slot, (t, _) in enumerate(items):
                where[(t, owner)] = owner * DEPTH + slot
        row = []
        for t, (p, q) in enumerate(TILES):
            row.append(where[(t, place(*p(*d)))])
            if t >= 2:
                row.append(where[(t, place(*q(*d)))])
        rows.append(row)
    return np.array(rows, np.int32)


def fetch(value, role):
    return lax.ppermute(value, BLK, [(place(*role(*d)), place(*d)) for d in ALL])


def position():
    return tuple(lax.axis_index(name) for name in BLK)


def dot(a, b):
    return lax.dot_general(
        a, b, (((0,), (0,)), ((), ())), preferred_element_type=jnp.float32
    )


def product(p, q):
    tile = dot(p[0][: PARTS[0]], q[0][: PARTS[0]])
    for u, v in zip(p[1:], q[1:]):
        tile += dot(u[...], v[...])
    return tile


def parted(block):
    return tuple(block.at[pl.ds(at, n)] for at, n in zip(STARTS, PARTS))


def owns(carrier, block):
    row = carrier[0][PARTS[0] :].astype(jnp.float32)
    return jnp.max(jnp.where(row == block.astype(jnp.float32), 1.0, 0.0)) > 0.5


def writer(out, slot):
    def put(tile):
        out[:, pl.ds(slot * SLAB, SLAB)] = tile.reshape(N_BULK, SLAB, W)

    return put


def settle(carrier, rhs, block, put):
    kept = owns(carrier, place(*block))

    @pl.when(kept)
    def _():
        put(product(carrier, rhs))

    @pl.when(jnp.logical_not(kept))
    def _():
        put(product(rhs, carrier))


def squeeze(out, rows):
    most = jnp.max(jnp.abs(out[:, :rows]), axis=0)
    most = jnp.max(jnp.max(most, axis=0, keepdims=True), axis=1, keepdims=True)
    most = jnp.maximum(most, 1e-30)
    power = jnp.ceil(jnp.log2(jnp.broadcast_to(most, (SLAB, W))))
    rank = lax.axis_index("z") * H + lax.axis_index("h")
    spread = 1.0 + rank.astype(jnp.float32) / N_BULK
    by = (jnp.exp2(TOP - power) * spread)[:1]
    for k in range(N_BULK):
        out[k, :rows] = out[k, :rows] * by
    return power


def early_kernel(a, b, w, x1, x2, x3, out, mark):
    a, b, w = parted(a), parted(b), parted(w)
    me = position()
    x = (x1, x2, x3)
    writer(out, 0)(product(a, a))
    writer(out, 1)(product(a, b))
    settle(x, a, own(*me), writer(out, 2))
    settle(x, b, sib(*me), writer(out, 3))
    settle(x, w, left(*me), writer(out, 4))
    mark[...] = squeeze(out, EARLY * SLAB)


def late_kernel(a, b, w, x1, x2, x3, v1, v2, v3, mark, out):
    a, b, w = parted(a), parted(b), parted(w)
    me = position()
    x, v = (x1, x2, x3), (v1, v2, v3)
    settle(v, x, right(*me), writer(out, 0))
    settle(v, a, own(*me), writer(out, 1))
    settle(v, b, sib(*me), writer(out, 2))
    settle(v, w, left(*me), writer(out, 3))
    power = squeeze(out, LATE * SLAB)
    first = lax.broadcasted_iota(jnp.int32, (SLAB, W), 0) < SLAB // 2
    power = jnp.where(first, mark[...], power)
    for k in range(N_BULK):
        out[k, LATE * SLAB :] = power


def pack_kernel(stamp, early, late, out):
    me = place(*position())
    k = 0
    for t in range(SLOTS):
        if t < EARLY:
            tile = early[pl.ds(t * SLAB, SLAB)]
        else:
            tile = late[pl.ds((t - EARLY) * SLAB, SLAB)]
        for _ in range(1 if t < 2 else 2):
            out[stamp[me, k]] = tile
            k += 1


def pick_kernel(table, cols, got, out):
    me = place(*position())
    for j in range(SLOTS):
        b = cols[0, j]
        slab = got[table[me, jnp.maximum(b, 0)]]
        out[j] = jnp.where(b >= 0, slab, 0.0)


def call(kernel, shapes, n_smem, n_tiles, *ins):
    vmem = pl.BlockSpec(memory_space=pltpu.VMEM)
    smem = pl.BlockSpec(memory_space=pltpu.SMEM)
    size = sum(int(np.prod(shape)) for shape in shapes)
    return pl.pallas_call(
        kernel,
        out_shape=[jax.ShapeDtypeStruct(shape, jnp.float32) for shape in shapes],
        in_specs=[smem] * n_smem + [vmem] * (len(ins) - n_smem),
        out_specs=[vmem] * len(shapes),
        compiler_params=pltpu.CompilerParams(vmem_limit_bytes=24 * 2**20),
        cost_estimate=pl.CostEstimate(
            flops=n_tiles * 2 * W * W * K,
            bytes_accessed=4 * size + sum(v.size * v.dtype.itemsize for v in ins),
            transcendentals=0,
        ),
    )(*ins)


def everywhere(value, axes):
    return lax.all_to_all(value, axes, 0, 0, tiled=True)


def total(got, power):
    spread = 1.0 + lax.broadcasted_iota(jnp.float32, (N_BULK, 1, 1), 0) / N_BULK
    by = jnp.exp2(power.astype(jnp.float32) - TOP) / spread
    return (got.astype(jnp.float32) * by).sum(0)


def local(aux_factors, tile_cols):
    row = jnp.pad(
        tile_cols.astype(jnp.bfloat16),
        ((0, 15), (0, W - SLOTS)),
        constant_values=-2,
    )
    a = aux_factors.reshape(K, W)
    send = [a[at : at + n] for at, n in zip(STARTS, PARTS)]
    send[0] = jnp.concatenate([send[0], row])
    x = [fetch(part, right) for part in send]
    w = fetch(a, left)
    b = fetch(a, sib)
    v = [fetch(part, diag_via) for part in x]

    shape = (N_BULK, EARLY * SLAB, W)
    early, mark = call(early_kernel, [shape, (SLAB, W)], 0, EARLY, a, b, w, *x)
    shape = (N_BULK, (LATE + 1) * SLAB, W)
    (late,) = call(late_kernel, [shape], 0, LATE, a, b, w, *x, *v, mark)
    parts = jnp.concatenate([early, late], 1).astype(jnp.float16)
    got = everywhere(parts, BULK)
    at, end = EARLY * SLAB, SLOTS * SLAB
    early = total(got[:, :at], got[:, end : end + 1, :1])
    late = total(got[:, at:end], got[:, -1:, :1])

    shape = (N_BLK * DEPTH, SLAB, W)
    (mail,) = call(pack_kernel, [shape], 1, 0, jnp.asarray(stamps()), early, late)
    mail = everywhere(mail, BLK)
    table = jnp.asarray(addresses())
    return call(pick_kernel, [(SLOTS, SLAB, W)], 2, 0, table, tile_cols, mail)[0]


def solution(mesh):
    fine = Mesh(mesh.devices.reshape(Z, H, L, X, C), (*BULK, *BLK))
    in_specs = (P(BULK, None, BLK), P(BLK, None))
    out_specs = P(BLK, BULK, None)
    return jax.shard_map(
        local, mesh=fine, in_specs=in_specs, out_specs=out_specs, check_vma=False
    )
```

```python
import jax
import jax.numpy as jnp
import numpy as np
from jax import lax
from jax.experimental import pallas as pl
from jax.experimental.pallas import tpu as pltpu
from jax.sharding import Mesh
from jax.sharding import PartitionSpec as P

Z, H, L, X, C = 8, 4, 2, 4, 2
BLK = ("l", "x", "c")
N_BLK, N_BULK = L * X * C, Z * H
BULK = ("z", "h")
SLOTS = 9
W = 256
K = 2048
PARTS = (1040, 1008)
STARTS = (0, 1040)
HALF = W // 2
SLAB = W // N_BULK
DEPTH = 4
TOP = 14.0


def place(l, x, c):
    return (l * X + x) * C + c


def own(l, x, c):
    return (l, x, c)


def sib(l, x, c):
    return (l, x, 1 - c)


def right(l, x, c):
    return (l, (x + 1) & 3, c)


def left(l, x, c):
    return (l, (x + 3) & 3, c ^ l ^ (x >> 1))


def diag(l, x, c):
    return (1 - l, (x + 1) & 3, c ^ l)


def diag_via(l, x, c):
    return (1 - l, x, c ^ l)


ALL = [(l, x, c) for l in range(L) for x in range(X) for c in range(C)]
TILES = [
    (own, own),
    (own, sib),
    (right, own),
    (right, sib),
    (right, left),
    (diag, right),
    (diag, own),
    (diag, sib),
    (diag, left),
]
EARLY, LATE = 5, 4


def ends(t, device):
    p, q = (place(*role(*device)) for role in TILES[t])
    return [(p, q)] if p == q else [(p, q), (q, p)]


def mailing(device):
    out = {}
    for t in range(SLOTS):
        for owner, other in ends(t, device):
            out.setdefault(owner, []).append((t, other))
    return out


def addresses():
    table = np.full((N_BLK, N_BLK + 1), -1, np.int32)
    for d in ALL:
        for owner, items in mailing(d).items():
            assert len(items) <= DEPTH
            for slot, (t, other) in enumerate(items):
                column = N_BLK if t == 1 and d[2] == 1 else other
                assert table[owner, column] < 0
                table[owner, column] = place(*d) * DEPTH + slot
    assert (table >= 0).all()
    return table


def stamps():
    rows = []
    for d in ALL:
        sent = mailing(d)
        row = []
        for t in range(SLOTS):
            for owner, other in ends(t, d):
                row.append(owner * DEPTH + sent[owner].index((t, other)))
        rows.append(row)
    return np.array(rows, np.int32)


def fetch(value, role):
    return lax.ppermute(value, BLK, [(place(*role(*d)), place(*d)) for d in ALL])


def position():
    return tuple(lax.axis_index(name) for name in BLK)


def dot(a, b):
    return lax.dot_general(
        a, b, (((0,), (0,)), ((), ())), preferred_element_type=jnp.float32
    )


def product(p, q):
    tile = dot(p[0][...], q[0][...])
    for u, v, n in zip(p[1:], q[1:], PARTS[1:]):
        tile += dot(u[:n], v[:n])
    return tile


def parted(block):
    return tuple(block.at[pl.ds(at, n)] for at, n in zip(STARTS, PARTS))


def owns(carrier, block):
    row = carrier[-1][PARTS[-1] :].astype(jnp.float32)
    return jnp.max(jnp.where(row == block.astype(jnp.float32), 1.0, 0.0)) > 0.5


def writer(out, slot):
    def put(tile):
        out[:, pl.ds(slot * SLAB, SLAB)] = tile.reshape(N_BULK, SLAB, W)

    return put


def settle(carrier, rhs, block, put):
    kept = owns(carrier, place(*block))

    @pl.when(kept)
    def _():
        put(product(carrier, rhs))

    @pl.when(jnp.logical_not(kept))
    def _():
        put(product(rhs, carrier))


def peak(out, rows):
    return jnp.max(jnp.max(jnp.abs(out[:, rows]), axis=0), axis=0, keepdims=True)


def early_kernel(cols, a, b, w, x1, x2, v1, out, most):
    del v1
    a, b, w = parted(a), parted(b), parted(w)
    me = position()
    x = (x1, x2)
    writer(out, 0)(product(a, a))
    other = place(*sib(*me))
    mine = cols[0, 0] == other
    for j in range(1, SLOTS):
        mine = jnp.logical_or(mine, cols[0, j] == other)
    for core in range(C):
        lanes = pl.ds(core * HALF, HALF)
        for kept, lhs, rhs in ((True, a, b), (False, b, a)):

            @pl.when(jnp.logical_and(me[2] == core, mine == kept))
            def _():
                tile = product(lhs, [part.at[:, lanes] for part in rhs])
                out[:, SLAB : 2 * SLAB, :HALF] = tile.reshape(N_BULK, SLAB, HALF)

    out[:, SLAB : 2 * SLAB, HALF:] = jnp.zeros((N_BULK, SLAB, HALF), jnp.float32)
    settle(x, a, own(*me), writer(out, 2))
    settle(x, b, sib(*me), writer(out, 3))
    settle(x, w, left(*me), writer(out, 4))
    most[...] = jnp.broadcast_to(peak(out, slice(0, EARLY * SLAB)), (SLAB, W))


def late_kernel(a, b, w, x1, x2, v1, v2, early, most, out):
    a, b, w = parted(a), parted(b), parted(w)
    me = position()
    x, v = (x1, x2), (v1, v2)
    settle(v, x, right(*me), writer(out, 5))
    settle(v, a, own(*me), writer(out, 6))
    settle(v, b, sib(*me), writer(out, 7))
    settle(v, w, left(*me), writer(out, 8))

    n = EARLY * SLAB
    most = jnp.maximum(peak(out, slice(n, SLOTS * SLAB)), most[:1])
    most = jnp.maximum(jnp.max(most, axis=1, keepdims=True), 1e-30)
    power = jnp.ceil(jnp.log2(jnp.broadcast_to(most, (SLAB, W))))
    rank = lax.axis_index("z") * H + lax.axis_index("h")
    spread = 1.0 + rank.astype(jnp.float32) / N_BULK
    by = (jnp.exp2(TOP - power) * spread)[:1]
    for k in range(N_BULK):
        out[k, :n] = early[k] * by
        out[k, n:] = out[k, n:] * by
        out[k, SLAB : 2 * SLAB, HALF:] = power[:, HALF:]


def pack_kernel(stamp, done, out):
    me = place(*position())
    k = 0
    for t in range(SLOTS):
        tile = done[pl.ds(t * SLAB, SLAB)]
        for _ in range(1 if t == 0 else 2):
            out[stamp[me, k]] = tile
            k += 1


def pick_kernel(table, cols, got, out):
    me = position()
    other = place(*sib(*me))
    me = place(*me)
    halves = (got[table[me, other]], got[table[me, N_BLK]])
    halves = jnp.concatenate([half[:, :HALF] for half in halves], axis=1)
    for j in range(SLOTS):
        b = cols[0, j]
        slab = got[table[me, jnp.maximum(b, 0)]]
        slab = jnp.where(b == other, halves, slab)
        out[j] = jnp.where(b >= 0, slab, 0.0)


def call(kernel, shapes, n_smem, n_tiles, *ins):
    vmem = pl.BlockSpec(memory_space=pltpu.VMEM)
    smem = pl.BlockSpec(memory_space=pltpu.SMEM)
    size = sum(int(np.prod(shape)) for shape in shapes)
    return pl.pallas_call(
        kernel,
        out_shape=[jax.ShapeDtypeStruct(shape, jnp.float32) for shape in shapes],
        in_specs=[smem] * n_smem + [vmem] * (len(ins) - n_smem),
        out_specs=[vmem] * len(shapes),
        compiler_params=pltpu.CompilerParams(vmem_limit_bytes=24 * 2**20),
        cost_estimate=pl.CostEstimate(
            flops=n_tiles * 2 * W * W * K,
            bytes_accessed=4 * size + sum(v.size * v.dtype.itemsize for v in ins),
            transcendentals=0,
        ),
    )(*ins)


def everywhere(value, axes):
    return lax.all_to_all(value, axes, 0, 0, tiled=True)


def total(got):
    spread = 1.0 + lax.broadcasted_iota(jnp.float32, (N_BULK, 1, 1), 0) / N_BULK
    power = got[:, SLAB : SLAB + 1, HALF : HALF + 1].astype(jnp.float32)
    return (got.astype(jnp.float32) * (jnp.exp2(power - TOP) / spread)).sum(0)


def local(aux_factors, tile_cols):
    row = jnp.pad(
        tile_cols.astype(jnp.bfloat16),
        ((0, 15), (0, W - SLOTS)),
        constant_values=-2,
    )
    a = aux_factors.reshape(K, W)
    send = [a[at : at + n] for at, n in zip(STARTS, PARTS)]
    send[-1] = jnp.concatenate([send[-1], row])
    x = [fetch(part, right) for part in send]
    w = fetch(a, left)
    b = fetch(a, sib)
    v = [fetch(part, diag_via) for part in x]

    shapes = [(N_BULK, EARLY * SLAB, W), (SLAB, W)]
    early = call(early_kernel, shapes, 1, EARLY, tile_cols, a, b, w, *x, v[0])
    shapes = [(N_BULK, SLOTS * SLAB, W)]
    (parts,) = call(late_kernel, shapes, 0, LATE, a, b, w, *x, *v, *early)
    done = total(everywhere(parts.astype(jnp.float16), BULK))

    shapes = [(N_BLK * DEPTH, SLAB, W)]
    (mail,) = call(pack_kernel, shapes, 1, 0, jnp.asarray(stamps()), done)
    mail = everywhere(mail, BLK)
    table = jnp.asarray(addresses())
    return call(pick_kernel, [(SLOTS, SLAB, W)], 2, 0, table, tile_cols, mail)[0]


def solution(mesh):
    fine = Mesh(mesh.devices.reshape(Z, H, L, X, C), (*BULK, *BLK))
    in_specs = (P(BULK, None, BLK), P(BLK, None))
    out_specs = P(BLK, BULK, None)
    return jax.shard_map(
        local, mesh=fine, in_specs=in_specs, out_specs=out_specs, check_vma=False
    )
```

```python
import jax
import jax.numpy as jnp
import numpy as np
from jax import lax
from jax.experimental import pallas as pl
from jax.experimental.pallas import tpu as pltpu
from jax.sharding import Mesh
from jax.sharding import PartitionSpec as P

Z, H, L, X, C = 8, 4, 2, 4, 2
BLK = ("l", "x", "c")
N_BLK, N_BULK = L * X * C, Z * H
BULK = ("z", "h")
SLOTS = 9
W = 256
K = 2048
PARTS = (1040, 1008)
STARTS = (0, 1040)
HALF = W // 2
SLAB = W // N_BULK
TOP = 14.0


def place(l, x, c):
    return (l * X + x) * C + c


def own(l, x, c):
    return (l, x, c)


def sib(l, x, c):
    return (l, x, 1 - c)


def right(l, x, c):
    return (l, (x + 1) & 3, c)


def left(l, x, c):
    return (l, (x + 3) & 3, c ^ l ^ (x >> 1))


def diag(l, x, c):
    return (1 - l, (x + 1) & 3, c ^ l)


def diag_via(l, x, c):
    return (1 - l, x, c ^ l)


ALL = [(l, x, c) for l in range(L) for x in range(X) for c in range(C)]
TILES = [
    (own, own),
    (own, sib),
    (right, own),
    (right, sib),
    (right, left),
    (diag, right),
    (diag, own),
    (diag, sib),
    (diag, left),
]
EARLY, LATE = 5, 4


def ends(t, device):
    p, q = (place(*role(*device)) for role in TILES[t])
    return [(p, q)] if p == q else [(p, q), (q, p)]


MAIL = ((sib, (1, 3, 7)), (right, (2, 3, 4, 5)), (diag, (5, 6, 7, 8)), (left, (4, 8)))


def addresses():
    table = np.full((N_BLK, N_BLK + 1), -1, np.int32)

    def enter(owner, t, device, index):
        pair = [place(*role(*device)) for role in TILES[t]]
        if owner not in pair:
            return
        pair.remove(owner)
        column = N_BLK if t == 1 and device[2] == 1 else pair[0]
        assert table[owner, column] < 0
        table[owner, column] = index

    for d in ALL:
        for t in range(SLOTS):
            enter(place(*d), t, d, t)
        index = SLOTS
        for role, sent in MAIL:
            for t in sent:
                enter(place(*role(*d)), t, d, index)
                index += 1
    assert (table >= 0).all()
    return table


def fetch(value, role):
    return lax.ppermute(value, BLK, [(place(*role(*d)), place(*d)) for d in ALL])


def hand(value, role):
    return lax.ppermute(value, BLK, [(place(*d), place(*role(*d))) for d in ALL])


def position():
    return tuple(lax.axis_index(name) for name in BLK)


def dot(a, b):
    return lax.dot_general(
        a, b, (((0,), (0,)), ((), ())), preferred_element_type=jnp.float32
    )


def product(p, q):
    tile = dot(p[0][...], q[0][...])
    for u, v, n in zip(p[1:], q[1:], PARTS[1:]):
        tile += dot(u[:n], v[:n])
    return tile


def parted(block):
    return tuple(block.at[pl.ds(at, n)] for at, n in zip(STARTS, PARTS))


def owns(carrier, block):
    row = carrier[-1][PARTS[-1] :].astype(jnp.float32)
    return jnp.max(jnp.where(row == block.astype(jnp.float32), 1.0, 0.0)) > 0.5


def writer(out, slot):
    def put(tile):
        out[:, pl.ds(slot * SLAB, SLAB)] = tile.reshape(N_BULK, SLAB, W)

    return put


def settle(carrier, rhs, block, put):
    kept = owns(carrier, place(*block))

    @pl.when(kept)
    def _():
        put(product(carrier, rhs))

    @pl.when(jnp.logical_not(kept))
    def _():
        put(product(rhs, carrier))


def peak(out, rows):
    return jnp.max(jnp.max(jnp.abs(out[:, rows]), axis=0), axis=0, keepdims=True)


def early_kernel(cols, a, b, w, x1, x2, v1, out, most):
    del v1
    a, b, w = parted(a), parted(b), parted(w)
    me = position()
    x = (x1, x2)
    writer(out, 0)(product(a, a))
    other = place(*sib(*me))
    mine = cols[0, 0] == other
    for j in range(1, SLOTS):
        mine = jnp.logical_or(mine, cols[0, j] == other)
    for core in range(C):
        lanes = pl.ds(core * HALF, HALF)
        for kept, lhs, rhs in ((True, a, b), (False, b, a)):

            @pl.when(jnp.logical_and(me[2] == core, mine == kept))
            def _():
                tile = product(lhs, [part.at[:, lanes] for part in rhs])
                out[:, SLAB : 2 * SLAB, :HALF] = tile.reshape(N_BULK, SLAB, HALF)

    out[:, SLAB : 2 * SLAB, HALF:] = jnp.zeros((N_BULK, SLAB, HALF), jnp.float32)
    settle(x, a, own(*me), writer(out, 2))
    settle(x, b, sib(*me), writer(out, 3))
    settle(x, w, left(*me), writer(out, 4))
    most[...] = jnp.broadcast_to(peak(out, slice(0, EARLY * SLAB)), (SLAB, W))


def late_kernel(a, b, w, x1, x2, v1, v2, early, most, out):
    a, b, w = parted(a), parted(b), parted(w)
    me = position()
    x, v = (x1, x2), (v1, v2)
    settle(v, x, right(*me), writer(out, 5))
    settle(v, a, own(*me), writer(out, 6))
    settle(v, b, sib(*me), writer(out, 7))
    settle(v, w, left(*me), writer(out, 8))

    n = EARLY * SLAB
    most = jnp.maximum(peak(out, slice(n, SLOTS * SLAB)), most[:1])
    most = jnp.maximum(jnp.max(most, axis=1, keepdims=True), 1e-30)
    power = jnp.ceil(jnp.log2(jnp.broadcast_to(most, (SLAB, W))))
    rank = lax.axis_index("z") * H + lax.axis_index("h")
    spread = 1.0 + rank.astype(jnp.float32) / N_BULK
    by = (jnp.exp2(TOP - power) * spread)[:1]
    for k in range(N_BULK):
        out[k, :n] = early[k] * by
        out[k, n:] = out[k, n:] * by
        out[k, SLAB : 2 * SLAB, HALF:] = power[:, HALF:]


def pick_kernel(table, cols, *refs):
    *parts, out, got = refs
    at = 0
    for part in parts:
        n = part.shape[0] // SLAB
        got[pl.ds(at, n)] = part[...].reshape(n, SLAB, W)
        at += n
    me = position()
    other = place(*sib(*me))
    me = place(*me)
    halves = (got[table[me, other]], got[table[me, N_BLK]])
    halves = jnp.concatenate([half[:, :HALF] for half in halves], axis=1)
    for j in range(SLOTS):
        b = cols[0, j]
        slab = got[table[me, jnp.maximum(b, 0)]]
        slab = jnp.where(b == other, halves, slab)
        out[j] = jnp.where(b >= 0, slab, 0.0)


def call(kernel, shapes, n_smem, n_tiles, *ins, scratch=()):
    vmem = pl.BlockSpec(memory_space=pltpu.VMEM)
    smem = pl.BlockSpec(memory_space=pltpu.SMEM)
    size = sum(int(np.prod(shape)) for shape in shapes)
    return pl.pallas_call(
        kernel,
        out_shape=[jax.ShapeDtypeStruct(shape, jnp.float32) for shape in shapes],
        in_specs=[smem] * n_smem + [vmem] * (len(ins) - n_smem),
        out_specs=[vmem] * len(shapes),
        scratch_shapes=[pltpu.VMEM(shape, jnp.float32) for shape in scratch],
        compiler_params=pltpu.CompilerParams(vmem_limit_bytes=24 * 2**20),
        cost_estimate=pl.CostEstimate(
            flops=n_tiles * 2 * W * W * K,
            bytes_accessed=4 * size + sum(v.size * v.dtype.itemsize for v in ins),
            transcendentals=0,
        ),
    )(*ins)


def everywhere(value, axes):
    return lax.all_to_all(value, axes, 0, 0, tiled=True)


def total(got):
    spread = 1.0 + lax.broadcasted_iota(jnp.float32, (N_BULK, 1, 1), 0) / N_BULK
    power = got[:, SLAB : SLAB + 1, HALF : HALF + 1].astype(jnp.float32)
    return (got.astype(jnp.float32) * (jnp.exp2(power - TOP) / spread)).sum(0)


def local(aux_factors, tile_cols):
    row = jnp.pad(
        tile_cols.astype(jnp.bfloat16),
        ((0, 15), (0, W - SLOTS)),
        constant_values=-2,
    )
    a = aux_factors.reshape(K, W)
    send = [a[at : at + n] for at, n in zip(STARTS, PARTS)]
    send[-1] = jnp.concatenate([send[-1], row])
    x = [fetch(part, right) for part in send]
    w = fetch(a, left)
    b = fetch(a, sib)
    v = [fetch(part, diag_via) for part in x]

    shapes = [(N_BULK, EARLY * SLAB, W), (SLAB, W)]
    early = call(early_kernel, shapes, 1, EARLY, tile_cols, a, b, w, *x, v[0])
    shapes = [(N_BULK, SLOTS * SLAB, W)]
    (parts,) = call(late_kernel, shapes, 0, LATE, a, b, w, *x, *v, *early)
    done = total(everywhere(parts.astype(jnp.float16), BULK))

    parts = [done]
    for role, sent in MAIL:
        slabs = [done[t * SLAB : (t + 1) * SLAB] for t in sent]
        parts.append(hand(jnp.concatenate(slabs), role))
    count = sum(part.shape[0] for part in parts) // SLAB
    return call(
        pick_kernel,
        [(SLOTS, SLAB, W)],
        2,
        0,
        jnp.asarray(addresses()),
        tile_cols,
        *parts,
        scratch=[(count, SLAB, W)],
    )[0]


def solution(mesh):
    fine = Mesh(mesh.devices.reshape(Z, H, L, X, C), (*BULK, *BLK))
    in_specs = (P(BULK, None, BLK), P(BLK, None))
    out_specs = P(BLK, BULK, None)
    return jax.shard_map(
        local, mesh=fine, in_specs=in_specs, out_specs=out_specs, check_vma=False
    )
```

```python
import jax
import jax.numpy as jnp
import numpy as np
from jax import lax
from jax.experimental import pallas as pl
from jax.experimental.pallas import tpu as pltpu
from jax.sharding import Mesh
from jax.sharding import PartitionSpec as P

Z, H, L, X, C = 8, 4, 2, 4, 2
BLK = ("l", "x", "c")
N_BLK, N_BULK = L * X * C, Z * H
BULK = ("z", "h")
SLOTS = 9
W = 256
K = 2048
PARTS = (1040, 1008)
STARTS = (0, 1040)
HALF = W // 2
SLAB = W // N_BULK
FIRST, SECOND = 8, 4
TOP = 14.0


def place(l, x, c):
    return (l * X + x) * C + c


def own(l, x, c):
    return (l, x, c)


def sib(l, x, c):
    return (l, x, 1 - c)


def right(l, x, c):
    return (l, (x + 1) & 3, c)


def left(l, x, c):
    return (l, (x + 3) & 3, c ^ l ^ (x >> 1))


def diag(l, x, c):
    return (1 - l, (x + 1) & 3, c ^ l)


def diag_via(l, x, c):
    return (1 - l, x, c ^ l)


ALL = [(l, x, c) for l in range(L) for x in range(X) for c in range(C)]
TILES = [
    (own, own),
    (own, sib),
    (right, own),
    (right, sib),
    (right, left),
    (diag, right),
    (diag, own),
    (diag, sib),
    (diag, left),
]
EARLY, LATE = 5, 4


def ends(t, device):
    p, q = (place(*role(*device)) for role in TILES[t])
    return [(p, q)] if p == q else [(p, q), (q, p)]


MAIL = ((sib, (1, 3, 7)), (right, (2, 3, 4, 5)), (diag, (5, 6, 7, 8)), (left, (4, 8)))


def addresses():
    table = np.full((N_BLK, N_BLK + 1), -1, np.int32)

    def enter(owner, t, device, index):
        pair = [place(*role(*device)) for role in TILES[t]]
        if owner not in pair:
            return
        pair.remove(owner)
        column = N_BLK if t == 1 and device[2] == 1 else pair[0]
        assert table[owner, column] < 0
        table[owner, column] = index

    for d in ALL:
        for t in range(SLOTS):
            enter(place(*d), t, d, t)
        index = SLOTS
        for role, sent in MAIL:
            for t in sent:
                enter(place(*role(*d)), t, d, index)
                index += 1
    assert (table >= 0).all()
    return table


def fetch(value, role):
    return lax.ppermute(value, BLK, [(place(*role(*d)), place(*d)) for d in ALL])


def hand(value, role):
    return lax.ppermute(value, BLK, [(place(*d), place(*role(*d))) for d in ALL])


def position():
    return tuple(lax.axis_index(name) for name in BLK)


def dot(a, b):
    return lax.dot_general(
        a, b, (((0,), (0,)), ((), ())), preferred_element_type=jnp.float32
    )


def product(p, q):
    tile = dot(p[0][...], q[0][...])
    for u, v, n in zip(p[1:], q[1:], PARTS[1:]):
        tile += dot(u[:n], v[:n])
    return tile


def parted(block):
    return tuple(block.at[pl.ds(at, n)] for at, n in zip(STARTS, PARTS))


def owns(carrier, block):
    row = carrier[-1][PARTS[-1] :].astype(jnp.float32)
    return jnp.max(jnp.where(row == block.astype(jnp.float32), 1.0, 0.0)) > 0.5


def writer(out, slot):
    def put(tile):
        out[:, pl.ds(slot * SLAB, SLAB)] = tile.reshape(N_BULK, SLAB, W)

    return put


def settle(carrier, rhs, block, put):
    kept = owns(carrier, place(*block))

    @pl.when(kept)
    def _():
        put(product(carrier, rhs))

    @pl.when(jnp.logical_not(kept))
    def _():
        put(product(rhs, carrier))


def peak(out, rows):
    return jnp.max(jnp.max(jnp.abs(out[:, rows]), axis=0), axis=0, keepdims=True)


def early_kernel(cols, a, b, w, x1, x2, v1, out, most):
    del v1
    a, b, w = parted(a), parted(b), parted(w)
    me = position()
    x = (x1, x2)
    writer(out, 0)(product(a, a))
    other = place(*sib(*me))
    mine = cols[0, 0] == other
    for j in range(1, SLOTS):
        mine = jnp.logical_or(mine, cols[0, j] == other)
    for core in range(C):
        lanes = pl.ds(core * HALF, HALF)
        for kept, lhs, rhs in ((True, a, b), (False, b, a)):

            @pl.when(jnp.logical_and(me[2] == core, mine == kept))
            def _():
                tile = product(lhs, [part.at[:, lanes] for part in rhs])
                out[:, SLAB : 2 * SLAB, :HALF] = tile.reshape(N_BULK, SLAB, HALF)

    out[:, SLAB : 2 * SLAB, HALF:] = jnp.zeros((N_BULK, SLAB, HALF), jnp.float32)
    settle(x, a, own(*me), writer(out, 2))
    settle(x, b, sib(*me), writer(out, 3))
    settle(x, w, left(*me), writer(out, 4))
    most[...] = jnp.broadcast_to(peak(out, slice(0, EARLY * SLAB)), (SLAB, W))


def late_kernel(a, b, w, x1, x2, v1, v2, early, most, out, late):
    a, b, w = parted(a), parted(b), parted(w)
    me = position()
    x, v = (x1, x2), (v1, v2)
    settle(v, x, right(*me), writer(late, 0))
    settle(v, a, own(*me), writer(late, 1))
    settle(v, b, sib(*me), writer(late, 2))
    settle(v, w, left(*me), writer(late, 3))

    most = jnp.maximum(peak(late, slice(0, LATE * SLAB)), most[:1])
    most = jnp.maximum(jnp.max(most, axis=1, keepdims=True), 1e-30)
    power = jnp.ceil(jnp.log2(jnp.broadcast_to(most, (SLAB, W))))
    z, h = lax.axis_index("z"), lax.axis_index("h")
    first = me[2] == 0
    rank = jnp.where(first, z, h * 2 + (z & 1))
    spread = 1.0 + rank.astype(jnp.float32) / FIRST
    by = (jnp.exp2(TOP - power) * spread)[:1]
    for z in range(Z):
        for h in range(H):
            k = z * H + h
            to = jnp.where(first, z, h * 2 + z % 2)
            at = pl.multiple_of(jnp.where(first, h, z // 2) * SLOTS * SLAB, SLAB)
            out[to, pl.ds(at, EARLY * SLAB)] = early[k] * by
            out[to, pl.ds(at + EARLY * SLAB, LATE * SLAB)] = late[k] * by
            out[to, pl.ds(at + SLAB, SLAB), HALF:] = power[:, HALF:]


def pick_kernel(table, cols, *refs):
    *parts, out, got = refs
    at = 0
    for part in parts:
        n = part.shape[0] // SLAB
        got[pl.ds(at, n)] = part[...].reshape(n, SLAB, W)
        at += n
    me = position()
    other = place(*sib(*me))
    me = place(*me)
    halves = (got[table[me, other]], got[table[me, N_BLK]])
    halves = jnp.concatenate([half[:, :HALF] for half in halves], axis=1)
    for j in range(SLOTS):
        b = cols[0, j]
        slab = got[table[me, jnp.maximum(b, 0)]]
        slab = jnp.where(b == other, halves, slab)
        out[j] = jnp.where(b >= 0, slab, 0.0)


def call(kernel, shapes, n_smem, n_tiles, *ins, scratch=()):
    vmem = pl.BlockSpec(memory_space=pltpu.VMEM)
    smem = pl.BlockSpec(memory_space=pltpu.SMEM)
    size = sum(int(np.prod(shape)) for shape in shapes)
    return pl.pallas_call(
        kernel,
        out_shape=[jax.ShapeDtypeStruct(shape, jnp.float32) for shape in shapes],
        in_specs=[smem] * n_smem + [vmem] * (len(ins) - n_smem),
        out_specs=[vmem] * len(shapes),
        scratch_shapes=[pltpu.VMEM(shape, jnp.float32) for shape in scratch],
        compiler_params=pltpu.CompilerParams(vmem_limit_bytes=24 * 2**20),
        cost_estimate=pl.CostEstimate(
            flops=n_tiles * 2 * W * W * K,
            bytes_accessed=4 * size + sum(v.size * v.dtype.itemsize for v in ins),
            transcendentals=0,
        ),
    )(*ins)


def rounds():
    first, second = [], []

    def device(z, h, core, chip):
        return ((z * H + h) * N_BLK) + chip * C + core

    for chip in range(N_BLK // C):
        for h in range(H):
            first.append([device(z, h, 0, chip) for z in range(Z)])
            for q in range(2):
                second.append([device(z, h, 1, chip) for z in range(q, Z, 2)])
        for z in range(Z):
            second.append([device(z, h, 0, chip) for h in range(H)])
        for z in range(0, Z, 2):
            first.append([device(z + q, h, 1, chip) for h in range(H) for q in range(2)])
    return first, second


def exchange(value, groups):
    return lax.all_to_all(
        value, (*BULK, *BLK), 0, 0, axis_index_groups=groups, tiled=True
    )


def total(parts):
    first, second = rounds()
    got = exchange(parts.astype(jnp.float16), first)
    spread = 1.0 + lax.broadcasted_iota(jnp.float32, (FIRST, 1, 1), 0) / FIRST
    power = got[:, SLAB : SLAB + 1, HALF : HALF + 1].astype(jnp.float32)
    got = (got.astype(jnp.float32) * (jnp.exp2(power - TOP) / spread)).sum(0)
    return exchange(got.reshape(SECOND, SLOTS * SLAB, W), second).sum(0)


def local(aux_factors, tile_cols):
    row = jnp.pad(
        tile_cols.astype(jnp.bfloat16),
        ((0, 15), (0, W - SLOTS)),
        constant_values=-2,
    )
    a = aux_factors.reshape(K, W)
    send = [a[at : at + n] for at, n in zip(STARTS, PARTS)]
    send[-1] = jnp.concatenate([send[-1], row])
    x = [fetch(part, right) for part in send]
    w = fetch(a, left)
    b = fetch(a, sib)
    v = [fetch(part, diag_via) for part in x]

    shapes = [(N_BULK, EARLY * SLAB, W), (SLAB, W)]
    early = call(early_kernel, shapes, 1, EARLY, tile_cols, a, b, w, *x, v[0])
    shapes = [(FIRST, SECOND * SLOTS * SLAB, W)]
    scratch = [(N_BULK, LATE * SLAB, W)]
    ins = (a, b, w, *x, *v, *early)
    (parts,) = call(late_kernel, shapes, 0, LATE, *ins, scratch=scratch)
    done = total(parts)

    parts = [done]
    for role, sent in MAIL:
        slabs = [done[t * SLAB : (t + 1) * SLAB] for t in sent]
        parts.append(hand(jnp.concatenate(slabs), role))
    count = sum(part.shape[0] for part in parts) // SLAB
    return call(
        pick_kernel,
        [(SLOTS, SLAB, W)],
        2,
        0,
        jnp.asarray(addresses()),
        tile_cols,
        *parts,
        scratch=[(count, SLAB, W)],
    )[0]


def solution(mesh):
    fine = Mesh(mesh.devices.reshape(Z, H, L, X, C), (*BULK, *BLK))
    in_specs = (P(BULK, None, BLK), P(BLK, None))
    out_specs = P(BLK, BULK, None)
    return jax.shard_map(
        local, mesh=fine, in_specs=in_specs, out_specs=out_specs, check_vma=False
    )
```

```python
import jax
import jax.numpy as jnp
import numpy as np
from jax import lax
from jax.experimental import pallas as pl
from jax.experimental.pallas import tpu as pltpu
from jax.sharding import Mesh
from jax.sharding import PartitionSpec as P

Z, H, L, X, C = 8, 4, 2, 4, 2
BLK = ("l", "x", "c")
N_BLK, N_BULK = L * X * C, Z * H
BULK = ("z", "h")
SLOTS = 9
W = 256
K = 2048
PARTS = (1040, 1008)
STARTS = (0, 1040)
HALF = W // 2
SLAB = W // N_BULK
FIRST, SECOND = 8, 4
TOP = 14.0


def place(l, x, c):
    return (l * X + x) * C + c


def own(l, x, c):
    return (l, x, c)


def sib(l, x, c):
    return (l, x, 1 - c)


def right(l, x, c):
    return (l, (x + 1) & 3, c)


def left(l, x, c):
    return (l, (x + 3) & 3, c ^ l ^ (x >> 1))


def diag(l, x, c):
    return (1 - l, (x + 1) & 3, c ^ l)


def diag_via(l, x, c):
    return (1 - l, x, c ^ l)


ALL = [(l, x, c) for l in range(L) for x in range(X) for c in range(C)]
TILES = [
    (own, own),
    (own, sib),
    (right, own),
    (right, sib),
    (right, left),
    (diag, right),
    (diag, own),
    (diag, sib),
    (diag, left),
]
EARLY, LATE = 5, 4


def ends(t, device):
    p, q = (place(*role(*device)) for role in TILES[t])
    return [(p, q)] if p == q else [(p, q), (q, p)]


MAIL = ((sib, (1, 3, 7)), (right, (2, 3, 4, 5)), (diag, (5, 6, 7, 8)), (left, (4, 8)))


def addresses():
    table = np.full((N_BLK, N_BLK + 1), -1, np.int32)

    def enter(owner, t, device, index):
        pair = [place(*role(*device)) for role in TILES[t]]
        if owner not in pair:
            return
        pair.remove(owner)
        column = N_BLK if t == 1 and device[2] == 1 else pair[0]
        assert table[owner, column] < 0
        table[owner, column] = index

    for d in ALL:
        for t in range(SLOTS):
            enter(place(*d), t, d, t)
        index = SLOTS
        for role, sent in MAIL:
            for t in sent:
                enter(place(*role(*d)), t, d, index)
                index += 1
    assert (table >= 0).all()
    return table


def fetch(value, role):
    return lax.ppermute(value, BLK, [(place(*role(*d)), place(*d)) for d in ALL])


def hand(value, role):
    return lax.ppermute(value, BLK, [(place(*d), place(*role(*d))) for d in ALL])


def position():
    return tuple(lax.axis_index(name) for name in BLK)


def dot(a, b):
    return lax.dot_general(
        a, b, (((0,), (0,)), ((), ())), preferred_element_type=jnp.float32
    )


def product(p, q):
    tile = dot(p[0][...], q[0][...])
    for u, v, n in zip(p[1:], q[1:], PARTS[1:]):
        tile += dot(u[:n], v[:n])
    return tile


def parted(block):
    return tuple(block.at[pl.ds(at, n)] for at, n in zip(STARTS, PARTS))


def owned(carrier, *blocks):
    row = carrier[-1][PARTS[-1] :].astype(jnp.float32)
    bits = jnp.zeros_like(row)
    for k, block in enumerate(blocks):
        here = row == place(*block).astype(jnp.float32)
        bits = jnp.where(here, float(1 << k), bits)
    bits = jnp.sum(bits).astype(jnp.int32)
    return [(bits >> k) & 1 == 1 for k in range(len(blocks))]


def writer(out, slot):
    def put(tile):
        out[:, pl.ds(slot * SLAB, SLAB)] = tile.reshape(N_BULK, SLAB, W)

    return put


def settle(carrier, rhs, kept, put):
    @pl.when(kept)
    def _():
        put(product(carrier, rhs))

    @pl.when(jnp.logical_not(kept))
    def _():
        put(product(rhs, carrier))


def peak(out, rows):
    return jnp.max(jnp.max(jnp.abs(out[:, rows]), axis=0), axis=0, keepdims=True)


def early_kernel(cols, a, b, w, x1, x2, v1, out, most):
    del v1
    a, b, w = parted(a), parted(b), parted(w)
    me = position()
    x = (x1, x2)
    writer(out, 0)(product(a, a))
    other = place(*sib(*me))
    mine = cols[0, 0] == other
    for j in range(1, SLOTS):
        mine = jnp.logical_or(mine, cols[0, j] == other)
    for core in range(C):
        lanes = pl.ds(core * HALF, HALF)
        for kept, lhs, rhs in ((True, a, b), (False, b, a)):

            @pl.when(jnp.logical_and(me[2] == core, mine == kept))
            def _():
                tile = product(lhs, [part.at[:, lanes] for part in rhs])
                out[:, SLAB : 2 * SLAB, :HALF] = tile.reshape(N_BULK, SLAB, HALF)

    out[:, SLAB : 2 * SLAB, HALF:] = jnp.zeros((N_BULK, SLAB, HALF), jnp.float32)
    kept = owned(x, own(*me), sib(*me), left(*me))
    for slot, rhs in enumerate((a, b, w)):
        settle(x, rhs, kept[slot], writer(out, 2 + slot))
    most[...] = jnp.broadcast_to(peak(out, slice(0, EARLY * SLAB)), (SLAB, W))


def late_kernel(a, b, w, x1, x2, v1, v2, early, most, out, late):
    a, b, w = parted(a), parted(b), parted(w)
    me = position()
    x, v = (x1, x2), (v1, v2)
    kept = owned(v, right(*me), own(*me), sib(*me), left(*me))
    for slot, rhs in enumerate((x, a, b, w)):
        settle(v, rhs, kept[slot], writer(late, slot))

    most = jnp.maximum(peak(late, slice(0, LATE * SLAB)), most[:1])
    most = jnp.maximum(jnp.max(most, axis=1, keepdims=True), 1e-30)
    power = jnp.ceil(jnp.log2(jnp.broadcast_to(most, (SLAB, W))))
    z, h = lax.axis_index("z"), lax.axis_index("h")
    first = me[2] == 0
    rank = jnp.where(first, z, h * 2 + (z & 1))
    spread = 1.0 + rank.astype(jnp.float32) / FIRST
    by = (jnp.exp2(TOP - power) * spread)[:1]
    for z in range(Z):
        for h in range(H):
            k = z * H + h
            to = jnp.where(first, z, h * 2 + z % 2)
            at = pl.multiple_of(jnp.where(first, h, z // 2) * SLOTS * SLAB, SLAB)
            out[to, pl.ds(at, EARLY * SLAB)] = early[k] * by
            out[to, pl.ds(at + EARLY * SLAB, LATE * SLAB)] = late[k] * by
            out[to, pl.ds(at + SLAB, SLAB), HALF:] = power[:, HALF:]


def pick_kernel(table, cols, *refs):
    *parts, out, got = refs
    at = 0
    for part in parts:
        n = part.shape[0] // SLAB
        got[pl.ds(at, n)] = part[...].reshape(n, SLAB, W)
        at += n
    me = position()
    other = place(*sib(*me))
    me = place(*me)
    halves = (got[table[me, other]], got[table[me, N_BLK]])
    halves = jnp.concatenate([half[:, :HALF] for half in halves], axis=1)
    for j in range(SLOTS):
        b = cols[0, j]
        slab = got[table[me, jnp.maximum(b, 0)]]
        slab = jnp.where(b == other, halves, slab)
        out[j] = jnp.where(b >= 0, slab, 0.0)


def call(kernel, shapes, n_smem, n_tiles, *ins, scratch=()):
    vmem = pl.BlockSpec(memory_space=pltpu.VMEM)
    smem = pl.BlockSpec(memory_space=pltpu.SMEM)
    size = sum(int(np.prod(shape)) for shape in shapes)
    return pl.pallas_call(
        kernel,
        out_shape=[jax.ShapeDtypeStruct(shape, jnp.float32) for shape in shapes],
        in_specs=[smem] * n_smem + [vmem] * (len(ins) - n_smem),
        out_specs=[vmem] * len(shapes),
        scratch_shapes=[pltpu.VMEM(shape, jnp.float32) for shape in scratch],
        compiler_params=pltpu.CompilerParams(vmem_limit_bytes=24 * 2**20),
        cost_estimate=pl.CostEstimate(
            flops=n_tiles * 2 * W * W * K,
            bytes_accessed=4 * size + sum(v.size * v.dtype.itemsize for v in ins),
            transcendentals=0,
        ),
    )(*ins)


def rounds():
    first, second = [], []

    def device(z, h, core, chip):
        return ((z * H + h) * N_BLK) + chip * C + core

    for chip in range(N_BLK // C):
        for h in range(H):
            first.append([device(z, h, 0, chip) for z in range(Z)])
            for q in range(2):
                second.append([device(z, h, 1, chip) for z in range(q, Z, 2)])
        for z in range(Z):
            second.append([device(z, h, 0, chip) for h in range(H)])
        for z in range(0, Z, 2):
            first.append([device(z + q, h, 1, chip) for h in range(H) for q in range(2)])
    return first, second


def exchange(value, groups):
    return lax.all_to_all(
        value, (*BULK, *BLK), 0, 0, axis_index_groups=groups, tiled=True
    )


def total(parts):
    first, second = rounds()
    got = exchange(parts.astype(jnp.float16), first)
    spread = 1.0 + lax.broadcasted_iota(jnp.float32, (FIRST, 1, 1), 0) / FIRST
    power = got[:, SLAB : SLAB + 1, HALF : HALF + 1].astype(jnp.float32)
    got = (got.astype(jnp.float32) * (jnp.exp2(power - TOP) / spread)).sum(0)
    return exchange(got.reshape(SECOND, SLOTS * SLAB, W), second).sum(0)


def local(aux_factors, tile_cols):
    row = jnp.pad(
        tile_cols.astype(jnp.bfloat16),
        ((0, 15), (0, W - SLOTS)),
        constant_values=-2,
    )
    a = aux_factors.reshape(K, W)
    send = [a[at : at + n] for at, n in zip(STARTS, PARTS)]
    send[-1] = jnp.concatenate([send[-1], row])
    x = [fetch(part, right) for part in send]
    w = fetch(a, left)
    b = fetch(a, sib)
    v = [fetch(part, diag_via) for part in x]

    shapes = [(N_BULK, EARLY * SLAB, W), (SLAB, W)]
    early = call(early_kernel, shapes, 1, EARLY, tile_cols, a, b, w, *x, v[0])
    shapes = [(FIRST, SECOND * SLOTS * SLAB, W)]
    scratch = [(N_BULK, LATE * SLAB, W)]
    ins = (a, b, w, *x, *v, *early)
    (parts,) = call(late_kernel, shapes, 0, LATE, *ins, scratch=scratch)
    done = total(parts)

    parts = [done]
    for role, sent in MAIL:
        slabs = [done[t * SLAB : (t + 1) * SLAB] for t in sent]
        parts.append(hand(jnp.concatenate(slabs), role))
    count = sum(part.shape[0] for part in parts) // SLAB
    return call(
        pick_kernel,
        [(SLOTS, SLAB, W)],
        2,
        0,
        jnp.asarray(addresses()),
        tile_cols,
        *parts,
        scratch=[(count, SLAB, W)],
    )[0]


def solution(mesh):
    fine = Mesh(mesh.devices.reshape(Z, H, L, X, C), (*BULK, *BLK))
    in_specs = (P(BULK, None, BLK), P(BLK, None))
    out_specs = P(BLK, BULK, None)
    return jax.shard_map(
        local, mesh=fine, in_specs=in_specs, out_specs=out_specs, check_vma=False
    )
```

```python
import jax
import jax.numpy as jnp
import numpy as np
from jax import lax
from jax.experimental import pallas as pl
from jax.experimental.pallas import tpu as pltpu
from jax.sharding import Mesh
from jax.sharding import PartitionSpec as P

Z, H, L, X, C = 8, 4, 2, 4, 2
BLK = ("l", "x", "c")
N_BLK, N_BULK = L * X * C, Z * H
BULK = ("z", "h")
SLOTS = 9
W = 256
K = 2048
PARTS = (1040, 1008)
STARTS = (0, 1040)
HALF = W // 2
SLAB = W // N_BULK
FIRST, SECOND = 8, 4
TOP = 14.0


def place(l, x, c):
    return (l * X + x) * C + c


def own(l, x, c):
    return (l, x, c)


def sib(l, x, c):
    return (l, x, 1 - c)


def right(l, x, c):
    return (l, (x + 1) & 3, c)


def left(l, x, c):
    return (l, (x + 3) & 3, c ^ l ^ (x >> 1))


def diag(l, x, c):
    return (1 - l, (x + 1) & 3, c ^ l)


def diag_via(l, x, c):
    return (1 - l, x, c ^ l)


ALL = [(l, x, c) for l in range(L) for x in range(X) for c in range(C)]
TILES = [
    (own, own),
    (own, sib),
    (right, own),
    (right, sib),
    (right, left),
    (diag, right),
    (diag, own),
    (diag, sib),
    (diag, left),
]
EARLY, LATE = 5, 4


def ends(t, device):
    p, q = (place(*role(*device)) for role in TILES[t])
    return [(p, q)] if p == q else [(p, q), (q, p)]


MAIL = ((sib, (1, 3, 7)), (right, (2, 3, 4, 5)), (diag, (5, 6, 7, 8)), (left, (4, 8)))


def addresses():
    table = np.full((N_BLK, N_BLK + 1), -1, np.int32)

    def enter(owner, t, device, index):
        pair = [place(*role(*device)) for role in TILES[t]]
        if owner not in pair:
            return
        pair.remove(owner)
        column = N_BLK if t == 1 and device[2] == 1 else pair[0]
        assert table[owner, column] < 0
        table[owner, column] = index

    for d in ALL:
        for t in range(SLOTS):
            enter(place(*d), t, d, t)
        index = SLOTS
        for role, sent in MAIL:
            for t in sent:
                enter(place(*role(*d)), t, d, index)
                index += 1
    assert (table >= 0).all()
    return table


def fetch(value, role):
    return lax.ppermute(value, BLK, [(place(*role(*d)), place(*d)) for d in ALL])


def hand(value, role):
    return lax.ppermute(value, BLK, [(place(*d), place(*role(*d))) for d in ALL])


def position():
    return tuple(lax.axis_index(name) for name in BLK)


def dot(a, b):
    return lax.dot_general(
        a, b, (((0,), (0,)), ((), ())), preferred_element_type=jnp.float32
    )


def partial(p, q, k):
    n = PARTS[k]
    return dot(p[k][:n], q[k][:n])


def product(p, q):
    return partial(p, q, 0) + partial(p, q, 1)


def parted(block):
    return tuple(block.at[pl.ds(at, n)] for at, n in zip(STARTS, PARTS))


def owned(row, *blocks):
    row = row.astype(jnp.float32)
    bits = jnp.zeros_like(row)
    for k, block in enumerate(blocks):
        here = row == place(*block).astype(jnp.float32)
        bits = jnp.where(here, float(1 << k), bits)
    bits = jnp.sum(bits).astype(jnp.int32)
    return [(bits >> k) & 1 == 1 for k in range(len(blocks))]


def listed(cols, block):
    here = cols[0, 0] == place(*block)
    for j in range(1, SLOTS):
        here = jnp.logical_or(here, cols[0, j] == place(*block))
    return here


def writer(out, slot):
    def put(tile):
        out[:, pl.ds(slot * SLAB, SLAB)] = tile.reshape(N_BULK, SLAB, W)

    return put


def settle(lhs, rhs, kept, put, of=product):
    @pl.when(kept)
    def _():
        put(of(lhs, rhs))

    @pl.when(jnp.logical_not(kept))
    def _():
        put(of(rhs, lhs))


def peak(out, rows):
    return jnp.max(jnp.max(jnp.abs(out[:, rows]), axis=0), axis=0, keepdims=True)


def early_kernel(cols, a, b, w, x1, x2, v1, out, most, begun, flags):
    rows = [r[end:] for r, end in ((b, K), (w, K), (x2, PARTS[1]))]
    a, b, w = parted(a), parted(b), parted(w)
    me = position()
    x, v = (x1, x2), (v1,)
    writer(out, 0)(product(a, a))
    mine = listed(cols, sib(*me))
    for core in range(C):
        lanes = pl.ds(core * HALF, HALF)
        for kept, lhs, rhs in ((True, a, b), (False, b, a)):

            @pl.when(jnp.logical_and(me[2] == core, mine == kept))
            def _():
                tile = product(lhs, [part.at[:, lanes] for part in rhs])
                out[:, SLAB : 2 * SLAB, :HALF] = tile.reshape(N_BULK, SLAB, HALF)

    out[:, SLAB : 2 * SLAB, HALF:] = jnp.zeros((N_BULK, SLAB, HALF), jnp.float32)
    by_b, by_w = (owned(row, diag(*me))[0] for row in rows[:2])
    *kept, by_x = owned(rows[2], own(*me), sib(*me), left(*me), diag(*me))
    for slot, rhs in enumerate((a, b, w)):
        settle(x, rhs, kept[slot], writer(out, 2 + slot))
    others = (by_x, listed(cols, diag(*me)), by_b, by_w)
    for slot, (rhs, theirs) in enumerate(zip((x, a, b, w), others)):
        flags[0, slot] = theirs.astype(jnp.int32)
        settle(rhs, v, theirs, writer(begun, slot), lambda p, q: partial(p, q, 0))
    most[...] = jnp.broadcast_to(peak(out, slice(0, EARLY * SLAB)), (SLAB, W))


def late_kernel(flags, a, b, w, x2, v2, early, most, begun, out, late):
    a, b, w = parted(a), parted(b), parted(w)
    me = position()
    x, v = (None, x2), (None, v2)
    for slot, rhs in enumerate((x, a, b, w)):
        rows = pl.ds(slot * SLAB, SLAB)

        def put(tile):
            late[:, rows] = begun[:, rows] + tile.reshape(N_BULK, SLAB, W)

        settle(rhs, v, flags[0, slot] == 1, put, lambda p, q: partial(p, q, 1))

    most = jnp.maximum(peak(late, slice(0, LATE * SLAB)), most[:1])
    most = jnp.maximum(jnp.max(most, axis=1, keepdims=True), 1e-30)
    power = jnp.ceil(jnp.log2(jnp.broadcast_to(most, (SLAB, W))))
    z, h = lax.axis_index("z"), lax.axis_index("h")
    first = me[2] == 0
    rank = jnp.where(first, z, h * 2 + (z & 1))
    spread = 1.0 + rank.astype(jnp.float32) / FIRST
    by = (jnp.exp2(TOP - power) * spread)[:1]
    for z in range(Z):
        for h in range(H):
            k = z * H + h
            to = jnp.where(first, z, h * 2 + z % 2)
            at = pl.multiple_of(jnp.where(first, h, z // 2) * SLOTS * SLAB, SLAB)
            out[to, pl.ds(at, EARLY * SLAB)] = early[k] * by
            out[to, pl.ds(at + EARLY * SLAB, LATE * SLAB)] = late[k] * by
            out[to, pl.ds(at + SLAB, SLAB), HALF:] = power[:, HALF:]


def pick_kernel(table, cols, *refs):
    *parts, out, got = refs
    at = 0
    for part in parts:
        n = part.shape[0] // SLAB
        got[pl.ds(at, n)] = part[...].reshape(n, SLAB, W)
        at += n
    me = position()
    other = place(*sib(*me))
    me = place(*me)
    halves = (got[table[me, other]], got[table[me, N_BLK]])
    halves = jnp.concatenate([half[:, :HALF] for half in halves], axis=1)
    for j in range(SLOTS):
        b = cols[0, j]
        slab = got[table[me, jnp.maximum(b, 0)]]
        slab = jnp.where(b == other, halves, slab)
        out[j] = jnp.where(b >= 0, slab, 0.0)


def call(kernel, shapes, n_smem, n_tiles, *ins, scratch=(), n_flags=0):
    vmem = pl.BlockSpec(memory_space=pltpu.VMEM)
    smem = pl.BlockSpec(memory_space=pltpu.SMEM)
    size = sum(int(np.prod(shape)) for shape in shapes)
    out_shape = [jax.ShapeDtypeStruct(shape, jnp.float32) for shape in shapes]
    out_specs = [vmem] * len(shapes)
    if n_flags:
        out_shape.append(jax.ShapeDtypeStruct((1, n_flags), jnp.int32))
        out_specs.append(smem)
    return pl.pallas_call(
        kernel,
        out_shape=out_shape,
        in_specs=[smem] * n_smem + [vmem] * (len(ins) - n_smem),
        out_specs=out_specs,
        scratch_shapes=[pltpu.VMEM(shape, jnp.float32) for shape in scratch],
        compiler_params=pltpu.CompilerParams(vmem_limit_bytes=24 * 2**20),
        cost_estimate=pl.CostEstimate(
            flops=n_tiles * 2 * W * W * K,
            bytes_accessed=4 * size + sum(v.size * v.dtype.itemsize for v in ins),
            transcendentals=0,
        ),
    )(*ins)


def rounds():
    first, second = [], []

    def device(z, h, core, chip):
        return ((z * H + h) * N_BLK) + chip * C + core

    for chip in range(N_BLK // C):
        for h in range(H):
            first.append([device(z, h, 0, chip) for z in range(Z)])
            for q in range(2):
                second.append([device(z, h, 1, chip) for z in range(q, Z, 2)])
        for z in range(Z):
            second.append([device(z, h, 0, chip) for h in range(H)])
        for z in range(0, Z, 2):
            first.append([device(z + q, h, 1, chip) for h in range(H) for q in range(2)])
    return first, second


def exchange(value, groups):
    return lax.all_to_all(
        value, (*BULK, *BLK), 0, 0, axis_index_groups=groups, tiled=True
    )


def total(parts):
    first, second = rounds()
    got = exchange(parts.astype(jnp.float16), first)
    spread = 1.0 + lax.broadcasted_iota(jnp.float32, (FIRST, 1, 1), 0) / FIRST
    power = got[:, SLAB : SLAB + 1, HALF : HALF + 1].astype(jnp.float32)
    got = (got.astype(jnp.float32) * (jnp.exp2(power - TOP) / spread)).sum(0)
    return exchange(got.reshape(SECOND, SLOTS * SLAB, W), second).sum(0)


def local(aux_factors, tile_cols):
    row = jnp.pad(
        tile_cols.astype(jnp.bfloat16),
        ((0, 15), (0, W - SLOTS)),
        constant_values=-2,
    )
    a = aux_factors.reshape(K, W)
    rowed = jnp.concatenate([a, row])
    x = [fetch(part, right) for part in (a[: PARTS[0]], rowed[PARTS[0] :])]
    w = fetch(rowed, left)
    b = fetch(rowed, sib)
    v = [fetch(part, diag_via) for part in x]

    late_shape = (N_BULK, LATE * SLAB, W)
    shapes = [(N_BULK, EARLY * SLAB, W), (SLAB, W), late_shape]
    ins = (tile_cols, a, b, w, *x, v[0])
    *early, flags = call(early_kernel, shapes, 1, EARLY, *ins, n_flags=LATE)
    shapes = [(FIRST, SECOND * SLOTS * SLAB, W)]
    ins = (flags, a, b, w, x[1], v[1], *early)
    (parts,) = call(late_kernel, shapes, 1, LATE, *ins, scratch=[late_shape])
    done = total(parts)

    parts = [done]
    for role, sent in MAIL:
        slabs = [done[t * SLAB : (t + 1) * SLAB] for t in sent]
        parts.append(hand(jnp.concatenate(slabs), role))
    count = sum(part.shape[0] for part in parts) // SLAB
    return call(
        pick_kernel,
        [(SLOTS, SLAB, W)],
        2,
        0,
        jnp.asarray(addresses()),
        tile_cols,
        *parts,
        scratch=[(count, SLAB, W)],
    )[0]


def solution(mesh):
    fine = Mesh(mesh.devices.reshape(Z, H, L, X, C), (*BULK, *BLK))
    in_specs = (P(BULK, None, BLK), P(BLK, None))
    out_specs = P(BLK, BULK, None)
    return jax.shard_map(
        local, mesh=fine, in_specs=in_specs, out_specs=out_specs, check_vma=False
    )
```

```python
import jax
import jax.numpy as jnp
import numpy as np
from jax import lax
from jax.experimental import pallas as pl
from jax.experimental.pallas import tpu as pltpu
from jax.sharding import Mesh
from jax.sharding import PartitionSpec as P

Z, H, L, X, C = 8, 4, 2, 4, 2
BLK = ("l", "x", "c")
N_BLK, N_BULK = L * X * C, Z * H
BULK = ("z", "h")
SLOTS = 9
W = 256
K = 2048
PARTS = (1040, 1008)
STARTS = (0, 1040)
HALF = W // 2
SLAB = W // N_BULK
FIRST, SECOND = 8, 4
TOP = 14.0


def place(l, x, c):
    return (l * X + x) * C + c


def own(l, x, c):
    return (l, x, c)


def sib(l, x, c):
    return (l, x, 1 - c)


def right(l, x, c):
    return (l, (x + 1) & 3, c)


def left(l, x, c):
    return (l, (x + 3) & 3, c ^ l ^ (x >> 1))


def diag(l, x, c):
    return (1 - l, (x + 1) & 3, c ^ l)


def diag_via(l, x, c):
    return (1 - l, x, c ^ l)


ALL = [(l, x, c) for l in range(L) for x in range(X) for c in range(C)]
TILES = [
    (own, own),
    (own, sib),
    (right, own),
    (right, sib),
    (right, left),
    (diag, right),
    (diag, own),
    (diag, sib),
    (diag, left),
]
EARLY, LATE = 5, 4


def ends(t, device):
    p, q = (place(*role(*device)) for role in TILES[t])
    return [(p, q)] if p == q else [(p, q), (q, p)]


MAIL = ((sib, (1, 3, 7)), (right, (2, 3, 4, 5)), (diag, (5, 6, 7, 8)), (left, (4, 8)))


def addresses():
    table = np.full((N_BLK, N_BLK + 1), -1, np.int32)

    def enter(owner, t, device, index):
        pair = [place(*role(*device)) for role in TILES[t]]
        if owner not in pair:
            return
        pair.remove(owner)
        column = N_BLK if t == 1 and device[2] == 1 else pair[0]
        assert table[owner, column] < 0
        table[owner, column] = index

    for d in ALL:
        for t in range(SLOTS):
            enter(place(*d), t, d, t)
        index = SLOTS
        for role, sent in MAIL:
            for t in sent:
                enter(place(*role(*d)), t, d, index)
                index += 1
    assert (table >= 0).all()
    return table


def fetch(value, role):
    return lax.ppermute(value, BLK, [(place(*role(*d)), place(*d)) for d in ALL])


def hand(value, role):
    return lax.ppermute(value, BLK, [(place(*d), place(*role(*d))) for d in ALL])


def position():
    return tuple(lax.axis_index(name) for name in BLK)


def dot(a, b):
    return lax.dot_general(
        a, b, (((0,), (0,)), ((), ())), preferred_element_type=jnp.float32
    )


def partial(p, q, k):
    n = PARTS[k]
    return dot(p[k][:n], q[k][:n])


def product(p, q):
    return partial(p, q, 0) + partial(p, q, 1)


def parted(block):
    return tuple(block.at[pl.ds(at, n)] for at, n in zip(STARTS, PARTS))


def owned(row, *blocks):
    row = row.astype(jnp.float32)
    bits = jnp.zeros_like(row)
    for k, block in enumerate(blocks):
        here = row == place(*block).astype(jnp.float32)
        bits = jnp.where(here, float(1 << k), bits)
    bits = jnp.sum(bits).astype(jnp.int32)
    return [(bits >> k) & 1 == 1 for k in range(len(blocks))]


def listed(cols, block):
    here = cols[0, 0] == place(*block)
    for j in range(1, SLOTS):
        here = jnp.logical_or(here, cols[0, j] == place(*block))
    return here


def writer(out, slot):
    def put(tile):
        out[:, pl.ds(slot * SLAB, SLAB)] = tile.reshape(N_BULK, SLAB, W)

    return put


def settle(lhs, rhs, kept, put, of=product):
    @pl.when(kept)
    def _():
        put(of(lhs, rhs))

    @pl.when(jnp.logical_not(kept))
    def _():
        put(of(rhs, lhs))


def peak(out, rows):
    return jnp.max(jnp.max(jnp.abs(out[:, rows]), axis=0), axis=0, keepdims=True)


def early_kernel(cols, a, b, w, x1, x2, v1, out, most, begun, flags):
    rows = [r[end:] for r, end in ((b, K), (w, K), (x2, PARTS[1]))]
    a, b, w = parted(a), parted(b), parted(w)
    me = position()
    x, v = (x1, x2), (v1,)
    writer(out, 0)(product(a, a))
    mine = listed(cols, sib(*me))
    for core in range(C):
        lanes = pl.ds(core * HALF, HALF)
        for kept, lhs, rhs in ((True, a, b), (False, b, a)):

            @pl.when(jnp.logical_and(me[2] == core, mine == kept))
            def _():
                tile = product(lhs, [part.at[:, lanes] for part in rhs])
                out[:, SLAB : 2 * SLAB, :HALF] = tile.reshape(N_BULK, SLAB, HALF)

    out[:, SLAB : 2 * SLAB, HALF:] = jnp.zeros((N_BULK, SLAB, HALF), jnp.float32)
    by_b, by_w = (owned(row, diag(*me))[0] for row in rows[:2])
    *kept, by_x = owned(rows[2], own(*me), sib(*me), left(*me), diag(*me))
    for slot, rhs in enumerate((a, b, w)):
        settle(x, rhs, kept[slot], writer(out, 2 + slot))
    others = (by_x, listed(cols, diag(*me)), by_b, by_w)
    for slot, (rhs, theirs) in enumerate(zip((x, a, b, w), others)):
        flags[0, slot] = theirs.astype(jnp.int32)
        settle(rhs, v, theirs, writer(begun, slot), lambda p, q: partial(p, q, 0))
    most[...] = jnp.broadcast_to(peak(out, slice(0, EARLY * SLAB)), (SLAB, W))


def late_kernel(flags, a, b, w, x2, v2, early, most, begun, out, late):
    a, b, w = parted(a), parted(b), parted(w)
    me = position()
    x, v = (None, x2), (None, v2)
    for slot, rhs in enumerate((x, a, b, w)):
        rows = pl.ds(slot * SLAB, SLAB)

        def put(tile):
            late[:, rows] = begun[:, rows] + tile.reshape(N_BULK, SLAB, W)

        settle(rhs, v, flags[0, slot] == 1, put, lambda p, q: partial(p, q, 1))

    most = jnp.maximum(peak(late, slice(0, LATE * SLAB)), most[:1])
    most = jnp.maximum(jnp.max(most, axis=1, keepdims=True), 1e-30)
    power = jnp.ceil(jnp.log2(jnp.broadcast_to(most, (SLAB, W))))
    z, h = lax.axis_index("z"), lax.axis_index("h")
    first = me[2] == 1
    rank = jnp.where(first, z, h * 2 + (z & 1))
    spread = 1.0 + rank.astype(jnp.float32) / FIRST
    by = (jnp.exp2(TOP - power) * spread)[:1]
    for z in range(Z):
        for h in range(H):
            k = z * H + h
            to = jnp.where(first, z, h * 2 + z % 2)
            at = pl.multiple_of(jnp.where(first, h, z // 2) * SLOTS * SLAB, SLAB)
            out[to, pl.ds(at, EARLY * SLAB)] = early[k] * by
            out[to, pl.ds(at + EARLY * SLAB, LATE * SLAB)] = late[k] * by
            out[to, pl.ds(at + SLAB, SLAB), HALF:] = power[:, HALF:]


def pick_kernel(table, cols, *refs):
    *parts, out, got = refs
    at = 0
    for part in parts:
        n = part.shape[0] // SLAB
        got[pl.ds(at, n)] = part[...].reshape(n, SLAB, W)
        at += n
    me = position()
    other = place(*sib(*me))
    me = place(*me)
    halves = (got[table[me, other]], got[table[me, N_BLK]])
    halves = jnp.concatenate([half[:, :HALF] for half in halves], axis=1)
    for j in range(SLOTS):
        b = cols[0, j]
        slab = got[table[me, jnp.maximum(b, 0)]]
        slab = jnp.where(b == other, halves, slab)
        out[j] = jnp.where(b >= 0, slab, 0.0)


def call(kernel, shapes, n_smem, n_tiles, *ins, scratch=(), n_flags=0):
    vmem = pl.BlockSpec(memory_space=pltpu.VMEM)
    smem = pl.BlockSpec(memory_space=pltpu.SMEM)
    size = sum(int(np.prod(shape)) for shape in shapes)
    out_shape = [jax.ShapeDtypeStruct(shape, jnp.float32) for shape in shapes]
    out_specs = [vmem] * len(shapes)
    if n_flags:
        out_shape.append(jax.ShapeDtypeStruct((1, n_flags), jnp.int32))
        out_specs.append(smem)
    return pl.pallas_call(
        kernel,
        out_shape=out_shape,
        in_specs=[smem] * n_smem + [vmem] * (len(ins) - n_smem),
        out_specs=out_specs,
        scratch_shapes=[pltpu.VMEM(shape, jnp.float32) for shape in scratch],
        compiler_params=pltpu.CompilerParams(vmem_limit_bytes=24 * 2**20),
        cost_estimate=pl.CostEstimate(
            flops=n_tiles * 2 * W * W * K,
            bytes_accessed=4 * size + sum(v.size * v.dtype.itemsize for v in ins),
            transcendentals=0,
        ),
    )(*ins)


def rounds():
    first, second = [], []

    def device(z, h, core, chip):
        return ((z * H + h) * N_BLK) + chip * C + core

    for chip in range(N_BLK // C):
        for h in range(H):
            first.append([device(z, h, 1, chip) for z in range(Z)])
            for q in range(2):
                second.append([device(z, h, 0, chip) for z in range(q, Z, 2)])
        for z in range(Z):
            second.append([device(z, h, 1, chip) for h in range(H)])
        for z in range(0, Z, 2):
            first.append([device(z + q, h, 0, chip) for h in range(H) for q in range(2)])
    return first, second


def exchange(value, groups):
    return lax.all_to_all(
        value, (*BULK, *BLK), 0, 0, axis_index_groups=groups, tiled=True
    )


def total(parts):
    first, second = rounds()
    got = exchange(parts.astype(jnp.float16), first)
    spread = 1.0 + lax.broadcasted_iota(jnp.float32, (FIRST, 1, 1), 0) / FIRST
    power = got[:, SLAB : SLAB + 1, HALF : HALF + 1].astype(jnp.float32)
    got = (got.astype(jnp.float32) * (jnp.exp2(power - TOP) / spread)).sum(0)
    return exchange(got.reshape(SECOND, SLOTS * SLAB, W), second).sum(0)


def local(aux_factors, tile_cols):
    row = jnp.pad(
        tile_cols.astype(jnp.bfloat16),
        ((0, 15), (0, W - SLOTS)),
        constant_values=-2,
    )
    a = aux_factors.reshape(K, W)
    rowed = jnp.concatenate([a, row])
    x = [fetch(part, right) for part in (a[: PARTS[0]], rowed[PARTS[0] :])]
    w = fetch(rowed, left)
    b = fetch(rowed, sib)
    v = [fetch(part, diag_via) for part in x]

    late_shape = (N_BULK, LATE * SLAB, W)
    shapes = [(N_BULK, EARLY * SLAB, W), (SLAB, W), late_shape]
    ins = (tile_cols, a, b, w, *x, v[0])
    *early, flags = call(early_kernel, shapes, 1, EARLY, *ins, n_flags=LATE)
    shapes = [(FIRST, SECOND * SLOTS * SLAB, W)]
    ins = (flags, a, b, w, x[1], v[1], *early)
    (parts,) = call(late_kernel, shapes, 1, LATE, *ins, scratch=[late_shape])
    done = total(parts)

    parts = [done]
    for role, sent in MAIL:
        slabs = [done[t * SLAB : (t + 1) * SLAB] for t in sent]
        parts.append(hand(jnp.concatenate(slabs), role))
    count = sum(part.shape[0] for part in parts) // SLAB
    return call(
        pick_kernel,
        [(SLOTS, SLAB, W)],
        2,
        0,
        jnp.asarray(addresses()),
        tile_cols,
        *parts,
        scratch=[(count, SLAB, W)],
    )[0]


def solution(mesh):
    fine = Mesh(mesh.devices.reshape(Z, H, L, X, C), (*BULK, *BLK))
    in_specs = (P(BULK, None, BLK), P(BLK, None))
    out_specs = P(BLK, BULK, None)
    return jax.shard_map(
        local, mesh=fine, in_specs=in_specs, out_specs=out_specs, check_vma=False
    )
```

```python
import jax
import jax.numpy as jnp
import numpy as np
from jax import lax
from jax.experimental import pallas as pl
from jax.experimental.pallas import tpu as pltpu
from jax.sharding import Mesh
from jax.sharding import PartitionSpec as P

Z, H, L, X, C = 8, 4, 2, 4, 2
BLK = ("l", "x", "c")
N_BLK, N_BULK = L * X * C, Z * H
BULK = ("z", "h")
SLOTS = 9
W = 256
K = 2048
PARTS = (1040, 1008)
STARTS = (0, 1040)
HALF = W // 2
SLAB = W // N_BULK
FIRST, SECOND = 8, 4
TOP = 14.0


def place(l, x, c):
    return (l * X + x) * C + c


def own(l, x, c):
    return (l, x, c)


def sib(l, x, c):
    return (l, x, 1 - c)


def right(l, x, c):
    return (l, (x + 1) & 3, c)


def left(l, x, c):
    return (l, (x + 3) & 3, c ^ l ^ (x >> 1))


def diag(l, x, c):
    return (1 - l, (x + 1) & 3, c ^ l)


def diag_via(l, x, c):
    return (1 - l, x, c ^ l)


ALL = [(l, x, c) for l in range(L) for x in range(X) for c in range(C)]
TILES = [
    (own, own),
    (own, sib),
    (right, own),
    (right, sib),
    (right, left),
    (diag, right),
    (diag, own),
    (diag, sib),
    (diag, left),
]
EARLY, LATE = 5, 4


def ends(t, device):
    p, q = (place(*role(*device)) for role in TILES[t])
    return [(p, q)] if p == q else [(p, q), (q, p)]


MAIL = ((sib, (1, 3, 7)), (right, (2, 3, 4, 5)), (diag, (5, 6, 7, 8)), (left, (4, 8, None, None)))


def addresses():
    table = np.full((N_BLK, N_BLK + 1), -1, np.int32)

    def enter(owner, t, device, index):
        if t is None:
            return
        pair = [place(*role(*device)) for role in TILES[t]]
        if owner not in pair:
            return
        pair.remove(owner)
        column = N_BLK if t == 1 and device[2] == 1 else pair[0]
        assert table[owner, column] < 0
        table[owner, column] = index

    for d in ALL:
        for t in range(SLOTS):
            enter(place(*d), t, d, t)
        index = SLOTS
        for role, sent in MAIL:
            for t in sent:
                enter(place(*role(*d)), t, d, index)
                index += 1
    assert (table >= 0).all()
    return table


def fetch(value, role):
    return lax.ppermute(value, BLK, [(place(*role(*d)), place(*d)) for d in ALL])


def hand(value, role):
    return lax.ppermute(value, BLK, [(place(*d), place(*role(*d))) for d in ALL])


def position():
    return tuple(lax.axis_index(name) for name in BLK)


def dot(a, b):
    return lax.dot_general(
        a, b, (((0,), (0,)), ((), ())), preferred_element_type=jnp.float32
    )


def partial(p, q, k):
    n = PARTS[k]
    return dot(p[k][:n], q[k][:n])


def product(p, q):
    return partial(p, q, 0) + partial(p, q, 1)


def parted(block):
    return tuple(block.at[pl.ds(at, n)] for at, n in zip(STARTS, PARTS))


def owned(row, *blocks):
    row = row.astype(jnp.float32)
    bits = jnp.zeros_like(row)
    for k, block in enumerate(blocks):
        here = row == place(*block).astype(jnp.float32)
        bits = jnp.where(here, float(1 << k), bits)
    bits = jnp.sum(bits).astype(jnp.int32)
    return [(bits >> k) & 1 == 1 for k in range(len(blocks))]


def listed(cols, block):
    here = cols[0, 0] == place(*block)
    for j in range(1, SLOTS):
        here = jnp.logical_or(here, cols[0, j] == place(*block))
    return here


def writer(out, slot):
    def put(tile):
        out[:, pl.ds(slot * SLAB, SLAB)] = tile.reshape(N_BULK, SLAB, W)

    return put


def settle(lhs, rhs, kept, put, of=product):
    @pl.when(kept)
    def _():
        put(of(lhs, rhs))

    @pl.when(jnp.logical_not(kept))
    def _():
        put(of(rhs, lhs))


def peak(out, rows):
    return jnp.max(jnp.max(jnp.abs(out[:, rows]), axis=0), axis=0, keepdims=True)


def early_kernel(cols, a, b, w, x1, x2, v1, out, most, begun, flags):
    rows = [r[end:] for r, end in ((b, K), (w, K), (x2, PARTS[1]))]
    a, b, w = parted(a), parted(b), parted(w)
    me = position()
    x, v = (x1, x2), (v1,)
    writer(out, 0)(product(a, a))
    mine = listed(cols, sib(*me))
    for core in range(C):
        lanes = pl.ds(core * HALF, HALF)
        for kept, lhs, rhs in ((True, a, b), (False, b, a)):

            @pl.when(jnp.logical_and(me[2] == core, mine == kept))
            def _():
                tile = product(lhs, [part.at[:, lanes] for part in rhs])
                out[:, SLAB : 2 * SLAB, :HALF] = tile.reshape(N_BULK, SLAB, HALF)

    out[:, SLAB : 2 * SLAB, HALF:] = jnp.zeros((N_BULK, SLAB, HALF), jnp.float32)
    by_b, by_w = (owned(row, diag(*me))[0] for row in rows[:2])
    *kept, by_x = owned(rows[2], own(*me), sib(*me), left(*me), diag(*me))
    for slot, rhs in enumerate((a, b, w)):
        settle(x, rhs, kept[slot], writer(out, 2 + slot))
    others = (by_x, listed(cols, diag(*me)), by_b, by_w)
    for slot, (rhs, theirs) in enumerate(zip((x, a, b, w), others)):
        flags[0, slot] = theirs.astype(jnp.int32)
        settle(rhs, v, theirs, writer(begun, slot), lambda p, q: partial(p, q, 0))
    most[...] = jnp.broadcast_to(peak(out, slice(0, EARLY * SLAB)), (SLAB, W))


def late_kernel(flags, a, b, w, x2, v2, early, most, begun, out, late):
    a, b, w = parted(a), parted(b), parted(w)
    me = position()
    x, v = (None, x2), (None, v2)
    for slot, rhs in enumerate((x, a, b, w)):
        rows = pl.ds(slot * SLAB, SLAB)

        def put(tile):
            late[:, rows] = begun[:, rows] + tile.reshape(N_BULK, SLAB, W)

        settle(rhs, v, flags[0, slot] == 1, put, lambda p, q: partial(p, q, 1))

    most = jnp.maximum(peak(late, slice(0, LATE * SLAB)), most[:1])
    most = jnp.maximum(jnp.max(most, axis=1, keepdims=True), 1e-30)
    power = jnp.ceil(jnp.log2(jnp.broadcast_to(most, (SLAB, W))))
    z, h = lax.axis_index("z"), lax.axis_index("h")
    first = me[2] == 1
    rank = jnp.where(first, z, h * 2 + (z & 1))
    spread = 1.0 + rank.astype(jnp.float32) / FIRST
    by = (jnp.exp2(TOP - power) * spread)[:1]
    for z in range(Z):
        for h in range(H):
            k = z * H + h
            to = jnp.where(first, z, h * 2 + z % 2)
            at = pl.multiple_of(jnp.where(first, h, z // 2) * SLOTS * SLAB, SLAB)
            out[to, pl.ds(at, EARLY * SLAB)] = early[k] * by
            out[to, pl.ds(at + EARLY * SLAB, LATE * SLAB)] = late[k] * by
            out[to, pl.ds(at + SLAB, SLAB), HALF:] = power[:, HALF:]


def pick_kernel(table, cols, *refs):
    *parts, out, got = refs
    at = 0
    for part in parts:
        n = part.shape[0] // SLAB
        got[pl.ds(at, n)] = part[...].reshape(n, SLAB, W)
        at += n
    me = position()
    other = place(*sib(*me))
    me = place(*me)
    halves = (got[table[me, other]], got[table[me, N_BLK]])
    halves = jnp.concatenate([half[:, :HALF] for half in halves], axis=1)
    for j in range(SLOTS):
        b = cols[0, j]
        slab = got[table[me, jnp.maximum(b, 0)]]
        slab = jnp.where(b == other, halves, slab)
        out[j] = jnp.where(b >= 0, slab, 0.0)


def call(kernel, shapes, n_smem, n_tiles, *ins, scratch=(), n_flags=0):
    vmem = pl.BlockSpec(memory_space=pltpu.VMEM)
    smem = pl.BlockSpec(memory_space=pltpu.SMEM)
    size = sum(int(np.prod(shape)) for shape in shapes)
    out_shape = [jax.ShapeDtypeStruct(shape, jnp.float32) for shape in shapes]
    out_specs = [vmem] * len(shapes)
    if n_flags:
        out_shape.append(jax.ShapeDtypeStruct((1, n_flags), jnp.int32))
        out_specs.append(smem)
    return pl.pallas_call(
        kernel,
        out_shape=out_shape,
        in_specs=[smem] * n_smem + [vmem] * (len(ins) - n_smem),
        out_specs=out_specs,
        scratch_shapes=[pltpu.VMEM(shape, jnp.float32) for shape in scratch],
        compiler_params=pltpu.CompilerParams(vmem_limit_bytes=24 * 2**20),
        cost_estimate=pl.CostEstimate(
            flops=n_tiles * 2 * W * W * K,
            bytes_accessed=4 * size + sum(v.size * v.dtype.itemsize for v in ins),
            transcendentals=0,
        ),
    )(*ins)


def rounds():
    first, second = [], []

    def device(z, h, core, chip):
        return ((z * H + h) * N_BLK) + chip * C + core

    for chip in range(N_BLK // C):
        for h in range(H):
            first.append([device(z, h, 1, chip) for z in range(Z)])
            for q in range(2):
                second.append([device(z, h, 0, chip) for z in range(q, Z, 2)])
        for z in range(Z):
            second.append([device(z, h, 1, chip) for h in range(H)])
        for z in range(0, Z, 2):
            first.append([device(z + q, h, 0, chip) for h in range(H) for q in range(2)])
    return first, second


def exchange(value, groups):
    return lax.all_to_all(
        value, (*BULK, *BLK), 0, 0, axis_index_groups=groups, tiled=True
    )


def total(parts):
    first, second = rounds()
    got = exchange(parts.astype(jnp.float16), first)
    spread = 1.0 + lax.broadcasted_iota(jnp.float32, (FIRST, 1, 1), 0) / FIRST
    power = got[:, SLAB : SLAB + 1, HALF : HALF + 1].astype(jnp.float32)
    got = (got.astype(jnp.float32) * (jnp.exp2(power - TOP) / spread)).sum(0)
    return exchange(got.reshape(SECOND, SLOTS * SLAB, W), second).sum(0)


def local(aux_factors, tile_cols):
    row = jnp.pad(
        tile_cols.astype(jnp.bfloat16),
        ((0, 15), (0, W - SLOTS)),
        constant_values=-2,
    )
    a = aux_factors.reshape(K, W)
    rowed = jnp.concatenate([a, row])
    x = [fetch(part, right) for part in (a[: PARTS[0]], rowed[PARTS[0] :])]
    w = fetch(rowed, left)
    b = fetch(rowed, sib)
    v = [fetch(part, diag_via) for part in x]

    late_shape = (N_BULK, LATE * SLAB, W)
    shapes = [(N_BULK, EARLY * SLAB, W), (SLAB, W), late_shape]
    ins = (tile_cols, a, b, w, *x, v[0])
    *early, flags = call(early_kernel, shapes, 1, EARLY, *ins, n_flags=LATE)
    shapes = [(FIRST, SECOND * SLOTS * SLAB, W)]
    ins = (flags, a, b, w, x[1], v[1], *early)
    (parts,) = call(late_kernel, shapes, 1, LATE, *ins, scratch=[late_shape])
    done = total(parts)

    parts = [done]
    for role, sent in MAIL:
        sent = [t or 0 for t in sent]
        slabs = [done[t * SLAB : (t + 1) * SLAB] for t in sent]
        parts.append(hand(jnp.concatenate(slabs), role))
    count = sum(part.shape[0] for part in parts) // SLAB
    return call(
        pick_kernel,
        [(SLOTS, SLAB, W)],
        2,
        0,
        jnp.asarray(addresses()),
        tile_cols,
        *parts,
        scratch=[(count, SLAB, W)],
    )[0]


def solution(mesh):
    fine = Mesh(mesh.devices.reshape(Z, H, L, X, C), (*BULK, *BLK))
    in_specs = (P(BULK, None, BLK), P(BLK, None))
    out_specs = P(BLK, BULK, None)
    return jax.shard_map(
        local, mesh=fine, in_specs=in_specs, out_specs=out_specs, check_vma=False
    )
```

```python
import jax
import jax.numpy as jnp
import numpy as np
from jax import lax
from jax.experimental import pallas as pl
from jax.experimental.pallas import tpu as pltpu
from jax.sharding import Mesh
from jax.sharding import PartitionSpec as P

Z, H, L, X, C = 8, 4, 2, 4, 2
BLK = ("l", "x", "c")
N_BLK, N_BULK = L * X * C, Z * H
BULK = ("z", "h")
SLOTS = 9
W = 256
K = 2048
PARTS = (1040, 1008)
STARTS = (0, 1040)
HALF = W // 2
SLAB = W // N_BULK
FIRST, SECOND = 8, 4
TOP = 14.0


def place(l, x, c):
    return (l * X + x) * C + c


def own(l, x, c):
    return (l, x, c)


def sib(l, x, c):
    return (l, x, 1 - c)


def right(l, x, c):
    return (l, (x + 1) & 3, c)


def left(l, x, c):
    return (l, (x + 3) & 3, c ^ l ^ (x >> 1))


def diag(l, x, c):
    return (1 - l, (x + 1) & 3, c ^ l)


def diag_via(l, x, c):
    return (1 - l, x, c ^ l)


ALL = [(l, x, c) for l in range(L) for x in range(X) for c in range(C)]
TILES = [
    (own, own),
    (own, sib),
    (right, own),
    (right, sib),
    (right, left),
    (diag, right),
    (diag, own),
    (diag, sib),
    (diag, left),
]
EARLY, LATE = 5, 4


def ends(t, device):
    p, q = (place(*role(*device)) for role in TILES[t])
    return [(p, q)] if p == q else [(p, q), (q, p)]


MAIL = ((sib, (1, 3, 7)), (right, (2, 3, 4, 5, None)), (diag, (5, 6, 7, 8, None)), (left, (4, 8, None, None)))


def addresses():
    table = np.full((N_BLK, N_BLK + 1), -1, np.int32)

    def enter(owner, t, device, index):
        if t is None:
            return
        pair = [place(*role(*device)) for role in TILES[t]]
        if owner not in pair:
            return
        pair.remove(owner)
        column = N_BLK if t == 1 and device[2] == 1 else pair[0]
        assert table[owner, column] < 0
        table[owner, column] = index

    for d in ALL:
        for t in range(SLOTS):
            enter(place(*d), t, d, t)
        index = SLOTS
        for role, sent in MAIL:
            for t in sent:
                enter(place(*role(*d)), t, d, index)
                index += 1
    assert (table >= 0).all()
    return table


def fetch(value, role):
    return lax.ppermute(value, BLK, [(place(*role(*d)), place(*d)) for d in ALL])


def hand(value, role):
    return lax.ppermute(value, BLK, [(place(*d), place(*role(*d))) for d in ALL])


def position():
    return tuple(lax.axis_index(name) for name in BLK)


def dot(a, b):
    return lax.dot_general(
        a, b, (((0,), (0,)), ((), ())), preferred_element_type=jnp.float32
    )


def partial(p, q, k):
    n = PARTS[k]
    return dot(p[k][:n], q[k][:n])


def product(p, q):
    return partial(p, q, 0) + partial(p, q, 1)


def parted(block):
    return tuple(block.at[pl.ds(at, n)] for at, n in zip(STARTS, PARTS))


def owned(row, *blocks):
    row = row.astype(jnp.float32)
    bits = jnp.zeros_like(row)
    for k, block in enumerate(blocks):
        here = row == place(*block).astype(jnp.float32)
        bits = jnp.where(here, float(1 << k), bits)
    bits = jnp.sum(bits).astype(jnp.int32)
    return [(bits >> k) & 1 == 1 for k in range(len(blocks))]


def listed(cols, block):
    here = cols[0, 0] == place(*block)
    for j in range(1, SLOTS):
        here = jnp.logical_or(here, cols[0, j] == place(*block))
    return here


def writer(out, slot):
    def put(tile):
        out[:, pl.ds(slot * SLAB, SLAB)] = tile.reshape(N_BULK, SLAB, W)

    return put


def settle(lhs, rhs, kept, put, of=product):
    @pl.when(kept)
    def _():
        put(of(lhs, rhs))

    @pl.when(jnp.logical_not(kept))
    def _():
        put(of(rhs, lhs))


def peak(out, rows):
    return jnp.max(jnp.max(jnp.abs(out[:, rows]), axis=0), axis=0, keepdims=True)


def early_kernel(cols, a, b, w, x1, x2, v1, out, most, begun, flags):
    rows = [r[end:] for r, end in ((b, K), (w, K), (x2, PARTS[1]))]
    a, b, w = parted(a), parted(b), parted(w)
    me = position()
    x, v = (x1, x2), (v1,)
    writer(out, 0)(product(a, a))
    mine = listed(cols, sib(*me))
    for core in range(C):
        lanes = pl.ds(core * HALF, HALF)
        for kept, lhs, rhs in ((True, a, b), (False, b, a)):

            @pl.when(jnp.logical_and(me[2] == core, mine == kept))
            def _():
                tile = product(lhs, [part.at[:, lanes] for part in rhs])
                out[:, SLAB : 2 * SLAB, :HALF] = tile.reshape(N_BULK, SLAB, HALF)

    out[:, SLAB : 2 * SLAB, HALF:] = jnp.zeros((N_BULK, SLAB, HALF), jnp.float32)
    by_b, by_w = (owned(row, diag(*me))[0] for row in rows[:2])
    *kept, by_x = owned(rows[2], own(*me), sib(*me), left(*me), diag(*me))
    for slot, rhs in enumerate((a, b, w)):
        settle(x, rhs, kept[slot], writer(out, 2 + slot))
    others = (by_x, listed(cols, diag(*me)), by_b, by_w)
    for slot, (rhs, theirs) in enumerate(zip((x, a, b, w), others)):
        flags[0, slot] = theirs.astype(jnp.int32)
        settle(rhs, v, theirs, writer(begun, slot), lambda p, q: partial(p, q, 0))
    most[...] = jnp.broadcast_to(peak(out, slice(0, EARLY * SLAB)), (SLAB, W))


def late_kernel(flags, a, b, w, x2, v2, early, most, begun, out, late):
    a, b, w = parted(a), parted(b), parted(w)
    me = position()
    x, v = (None, x2), (None, v2)
    for slot, rhs in enumerate((x, a, b, w)):
        rows = pl.ds(slot * SLAB, SLAB)

        def put(tile):
            late[:, rows] = begun[:, rows] + tile.reshape(N_BULK, SLAB, W)

        settle(rhs, v, flags[0, slot] == 1, put, lambda p, q: partial(p, q, 1))

    most = jnp.maximum(peak(late, slice(0, LATE * SLAB)), most[:1])
    most = jnp.maximum(jnp.max(most, axis=1, keepdims=True), 1e-30)
    power = jnp.ceil(jnp.log2(jnp.broadcast_to(most, (SLAB, W))))
    z, h = lax.axis_index("z"), lax.axis_index("h")
    first = me[2] == 1
    rank = jnp.where(first, z, h * 2 + (z & 1))
    spread = 1.0 + rank.astype(jnp.float32) / FIRST
    by = (jnp.exp2(TOP - power) * spread)[:1]
    for z in range(Z):
        for h in range(H):
            k = z * H + h
            to = jnp.where(first, z, h * 2 + z % 2)
            at = pl.multiple_of(jnp.where(first, h, z // 2) * SLOTS * SLAB, SLAB)
            out[to, pl.ds(at, EARLY * SLAB)] = early[k] * by
            out[to, pl.ds(at + EARLY * SLAB, LATE * SLAB)] = late[k] * by
            out[to, pl.ds(at + SLAB, SLAB), HALF:] = power[:, HALF:]


def pick_kernel(table, cols, *refs):
    *parts, out, got = refs
    at = 0
    for part in parts:
        n = part.shape[0] // SLAB
        got[pl.ds(at, n)] = part[...].reshape(n, SLAB, W)
        at += n
    me = position()
    other = place(*sib(*me))
    me = place(*me)
    halves = (got[table[me, other]], got[table[me, N_BLK]])
    halves = jnp.concatenate([half[:, :HALF] for half in halves], axis=1)
    for j in range(SLOTS):
        b = cols[0, j]
        slab = got[table[me, jnp.maximum(b, 0)]]
        slab = jnp.where(b == other, halves, slab)
        out[j] = jnp.where(b >= 0, slab, 0.0)


def call(kernel, shapes, n_smem, n_tiles, *ins, scratch=(), n_flags=0):
    vmem = pl.BlockSpec(memory_space=pltpu.VMEM)
    smem = pl.BlockSpec(memory_space=pltpu.SMEM)
    size = sum(int(np.prod(shape)) for shape in shapes)
    out_shape = [jax.ShapeDtypeStruct(shape, jnp.float32) for shape in shapes]
    out_specs = [vmem] * len(shapes)
    if n_flags:
        out_shape.append(jax.ShapeDtypeStruct((1, n_flags), jnp.int32))
        out_specs.append(smem)
    return pl.pallas_call(
        kernel,
        out_shape=out_shape,
        in_specs=[smem] * n_smem + [vmem] * (len(ins) - n_smem),
        out_specs=out_specs,
        scratch_shapes=[pltpu.VMEM(shape, jnp.float32) for shape in scratch],
        compiler_params=pltpu.CompilerParams(vmem_limit_bytes=24 * 2**20),
        cost_estimate=pl.CostEstimate(
            flops=n_tiles * 2 * W * W * K,
            bytes_accessed=4 * size + sum(v.size * v.dtype.itemsize for v in ins),
            transcendentals=0,
        ),
    )(*ins)


def rounds():
    first, second = [], []

    def device(z, h, core, chip):
        return ((z * H + h) * N_BLK) + chip * C + core

    for chip in range(N_BLK // C):
        for h in range(H):
            first.append([device(z, h, 1, chip) for z in range(Z)])
            for q in range(2):
                second.append([device(z, h, 0, chip) for z in range(q, Z, 2)])
        for z in range(Z):
            second.append([device(z, h, 1, chip) for h in range(H)])
        for z in range(0, Z, 2):
            first.append([device(z + q, h, 0, chip) for h in range(H) for q in range(2)])
    return first, second


def exchange(value, groups):
    return lax.all_to_all(
        value, (*BULK, *BLK), 0, 0, axis_index_groups=groups, tiled=True
    )


def total(parts):
    first, second = rounds()
    got = exchange(parts.astype(jnp.float16), first)
    spread = 1.0 + lax.broadcasted_iota(jnp.float32, (FIRST, 1, 1), 0) / FIRST
    power = got[:, SLAB : SLAB + 1, HALF : HALF + 1].astype(jnp.float32)
    got = (got.astype(jnp.float32) * (jnp.exp2(power - TOP) / spread)).sum(0)
    return exchange(got.reshape(SECOND, SLOTS * SLAB, W), second).sum(0)


def local(aux_factors, tile_cols):
    row = jnp.pad(
        tile_cols.astype(jnp.bfloat16),
        ((0, 15), (0, W - SLOTS)),
        constant_values=-2,
    )
    a = aux_factors.reshape(K, W)
    rowed = jnp.concatenate([a, row])
    x = [fetch(part, right) for part in (a[: PARTS[0]], rowed[PARTS[0] :])]
    w = fetch(rowed, left)
    b = fetch(rowed, sib)
    v = [fetch(part, diag_via) for part in x]

    late_shape = (N_BULK, LATE * SLAB, W)
    shapes = [(N_BULK, EARLY * SLAB, W), (SLAB, W), late_shape]
    ins = (tile_cols, a, b, w, *x, v[0])
    *early, flags = call(early_kernel, shapes, 1, EARLY, *ins, n_flags=LATE)
    shapes = [(FIRST, SECOND * SLOTS * SLAB, W)]
    ins = (flags, a, b, w, x[1], v[1], *early)
    (parts,) = call(late_kernel, shapes, 1, LATE, *ins, scratch=[late_shape])
    done = total(parts)

    parts = [done]
    for role, sent in MAIL:
        sent = [t or 0 for t in sent]
        slabs = [done[t * SLAB : (t + 1) * SLAB] for t in sent]
        parts.append(hand(jnp.concatenate(slabs), role))
    count = sum(part.shape[0] for part in parts) // SLAB
    return call(
        pick_kernel,
        [(SLOTS, SLAB, W)],
        2,
        0,
        jnp.asarray(addresses()),
        tile_cols,
        *parts,
        scratch=[(count, SLAB, W)],
    )[0]


def solution(mesh):
    fine = Mesh(mesh.devices.reshape(Z, H, L, X, C), (*BULK, *BLK))
    in_specs = (P(BULK, None, BLK), P(BLK, None))
    out_specs = P(BLK, BULK, None)
    return jax.shard_map(
        local, mesh=fine, in_specs=in_specs, out_specs=out_specs, check_vma=False
    )
```

```python
import jax
import jax.numpy as jnp
import numpy as np
from jax import lax
from jax.experimental import pallas as pl
from jax.experimental.pallas import tpu as pltpu
from jax.sharding import Mesh
from jax.sharding import PartitionSpec as P

Z, H, L, X, C = 8, 4, 2, 4, 2
BLK = ("l", "x", "c")
N_BLK, N_BULK = L * X * C, Z * H
BULK = ("z", "h")
SLOTS = 9
W = 256
K = 2048
PARTS = (1056, 992)
STARTS = (0, 1056)
HALF = W // 2
SLAB = W // N_BULK
FIRST, SECOND = 8, 4
TOP = 14.0


def place(l, x, c):
    return (l * X + x) * C + c


def own(l, x, c):
    return (l, x, c)


def sib(l, x, c):
    return (l, x, 1 - c)


def right(l, x, c):
    return (l, (x + 1) & 3, c)


def left(l, x, c):
    return (l, (x + 3) & 3, c ^ l ^ (x >> 1))


def diag(l, x, c):
    return (1 - l, (x + 1) & 3, c ^ l)


def diag_via(l, x, c):
    return (1 - l, x, c ^ l)


ALL = [(l, x, c) for l in range(L) for x in range(X) for c in range(C)]
TILES = [
    (own, own),
    (own, sib),
    (right, own),
    (right, sib),
    (right, left),
    (diag, right),
    (diag, own),
    (diag, sib),
    (diag, left),
]
EARLY, LATE = 5, 4


def ends(t, device):
    p, q = (place(*role(*device)) for role in TILES[t])
    return [(p, q)] if p == q else [(p, q), (q, p)]


MAIL = ((sib, (1, 3, 7)), (right, (2, 3, 4, 5)), (diag, (5, 6, 7, 8)), (left, (4, 8, None, None)))


def addresses():
    table = np.full((N_BLK, N_BLK + 1), -1, np.int32)

    def enter(owner, t, device, index):
        if t is None:
            return
        pair = [place(*role(*device)) for role in TILES[t]]
        if owner not in pair:
            return
        pair.remove(owner)
        column = N_BLK if t == 1 and device[2] == 1 else pair[0]
        assert table[owner, column] < 0
        table[owner, column] = index

    for d in ALL:
        for t in range(SLOTS):
            enter(place(*d), t, d, t)
        index = SLOTS
        for role, sent in MAIL:
            for t in sent:
                enter(place(*role(*d)), t, d, index)
                index += 1
    assert (table >= 0).all()
    return table


def fetch(value, role):
    return lax.ppermute(value, BLK, [(place(*role(*d)), place(*d)) for d in ALL])


def hand(value, role):
    return lax.ppermute(value, BLK, [(place(*d), place(*role(*d))) for d in ALL])


def position():
    return tuple(lax.axis_index(name) for name in BLK)


def dot(a, b):
    return lax.dot_general(
        a, b, (((0,), (0,)), ((), ())), preferred_element_type=jnp.float32
    )


def partial(p, q, k):
    n = PARTS[k]
    return dot(p[k][:n], q[k][:n])


def product(p, q):
    return partial(p, q, 0) + partial(p, q, 1)


def parted(block):
    return tuple(block.at[pl.ds(at, n)] for at, n in zip(STARTS, PARTS))


def owned(row, *blocks):
    row = row.astype(jnp.float32)
    bits = jnp.zeros_like(row)
    for k, block in enumerate(blocks):
        here = row == place(*block).astype(jnp.float32)
        bits = jnp.where(here, float(1 << k), bits)
    bits = jnp.sum(bits).astype(jnp.int32)
    return [(bits >> k) & 1 == 1 for k in range(len(blocks))]


def listed(cols, block):
    here = cols[0, 0] == place(*block)
    for j in range(1, SLOTS):
        here = jnp.logical_or(here, cols[0, j] == place(*block))
    return here


def writer(out, slot):
    def put(tile):
        out[:, pl.ds(slot * SLAB, SLAB)] = tile.reshape(N_BULK, SLAB, W)

    return put


def settle(lhs, rhs, kept, put, of=product):
    @pl.when(kept)
    def _():
        put(of(lhs, rhs))

    @pl.when(jnp.logical_not(kept))
    def _():
        put(of(rhs, lhs))


def peak(out, rows):
    return jnp.max(jnp.max(jnp.abs(out[:, rows]), axis=0), axis=0, keepdims=True)


def early_kernel(cols, a, b, w, x1, x2, v1, out, most, begun, flags):
    rows = [r[end:] for r, end in ((b, K), (w, K), (x2, PARTS[1]))]
    a, b, w = parted(a), parted(b), parted(w)
    me = position()
    x, v = (x1, x2), (v1,)
    writer(out, 0)(product(a, a))
    mine = listed(cols, sib(*me))
    for core in range(C):
        lanes = pl.ds(core * HALF, HALF)
        for kept, lhs, rhs in ((True, a, b), (False, b, a)):

            @pl.when(jnp.logical_and(me[2] == core, mine == kept))
            def _():
                tile = product(lhs, [part.at[:, lanes] for part in rhs])
                out[:, SLAB : 2 * SLAB, :HALF] = tile.reshape(N_BULK, SLAB, HALF)

    out[:, SLAB : 2 * SLAB, HALF:] = jnp.zeros((N_BULK, SLAB, HALF), jnp.float32)
    by_b, by_w = (owned(row, diag(*me))[0] for row in rows[:2])
    *kept, by_x = owned(rows[2], own(*me), sib(*me), left(*me), diag(*me))
    for slot, rhs in enumerate((a, b, w)):
        settle(x, rhs, kept[slot], writer(out, 2 + slot))
    others = (by_x, listed(cols, diag(*me)), by_b, by_w)
    for slot, (rhs, theirs) in enumerate(zip((x, a, b, w), others)):
        flags[0, slot] = theirs.astype(jnp.int32)
        settle(rhs, v, theirs, writer(begun, slot), lambda p, q: partial(p, q, 0))
    most[...] = jnp.broadcast_to(peak(out, slice(0, EARLY * SLAB)), (SLAB, W))


def late_kernel(flags, a, b, w, x2, v2, early, most, begun, out, late):
    a, b, w = parted(a), parted(b), parted(w)
    me = position()
    x, v = (None, x2), (None, v2)
    for slot, rhs in enumerate((x, a, b, w)):
        rows = pl.ds(slot * SLAB, SLAB)

        def put(tile):
            late[:, rows] = begun[:, rows] + tile.reshape(N_BULK, SLAB, W)

        settle(rhs, v, flags[0, slot] == 1, put, lambda p, q: partial(p, q, 1))

    most = jnp.maximum(peak(late, slice(0, LATE * SLAB)), most[:1])
    most = jnp.maximum(jnp.max(most, axis=1, keepdims=True), 1e-30)
    power = jnp.ceil(jnp.log2(jnp.broadcast_to(most, (SLAB, W))))
    z, h = lax.axis_index("z"), lax.axis_index("h")
    first = me[2] == 1
    rank = jnp.where(first, z, h * 2 + (z & 1))
    spread = 1.0 + rank.astype(jnp.float32) / FIRST
    by = (jnp.exp2(TOP - power) * spread)[:1]
    for z in range(Z):
        for h in range(H):
            k = z * H + h
            to = jnp.where(first, z, h * 2 + z % 2)
            at = pl.multiple_of(jnp.where(first, h, z // 2) * SLOTS * SLAB, SLAB)
            out[to, pl.ds(at, EARLY * SLAB)] = early[k] * by
            out[to, pl.ds(at + EARLY * SLAB, LATE * SLAB)] = late[k] * by
            out[to, pl.ds(at + SLAB, SLAB), HALF:] = power[:, HALF:]


def pick_kernel(table, cols, *refs):
    *parts, out, got = refs
    at = 0
    for part in parts:
        n = part.shape[0] // SLAB
        got[pl.ds(at, n)] = part[...].reshape(n, SLAB, W)
        at += n
    me = position()
    other = place(*sib(*me))
    me = place(*me)
    halves = (got[table[me, other]], got[table[me, N_BLK]])
    halves = jnp.concatenate([half[:, :HALF] for half in halves], axis=1)
    for j in range(SLOTS):
        b = cols[0, j]
        slab = got[table[me, jnp.maximum(b, 0)]]
        slab = jnp.where(b == other, halves, slab)
        out[j] = jnp.where(b >= 0, slab, 0.0)


def call(kernel, shapes, n_smem, n_tiles, *ins, scratch=(), n_flags=0):
    vmem = pl.BlockSpec(memory_space=pltpu.VMEM)
    smem = pl.BlockSpec(memory_space=pltpu.SMEM)
    size = sum(int(np.prod(shape)) for shape in shapes)
    out_shape = [jax.ShapeDtypeStruct(shape, jnp.float32) for shape in shapes]
    out_specs = [vmem] * len(shapes)
    if n_flags:
        out_shape.append(jax.ShapeDtypeStruct((1, n_flags), jnp.int32))
        out_specs.append(smem)
    return pl.pallas_call(
        kernel,
        out_shape=out_shape,
        in_specs=[smem] * n_smem + [vmem] * (len(ins) - n_smem),
        out_specs=out_specs,
        scratch_shapes=[pltpu.VMEM(shape, jnp.float32) for shape in scratch],
        compiler_params=pltpu.CompilerParams(vmem_limit_bytes=24 * 2**20),
        cost_estimate=pl.CostEstimate(
            flops=n_tiles * 2 * W * W * K,
            bytes_accessed=4 * size + sum(v.size * v.dtype.itemsize for v in ins),
            transcendentals=0,
        ),
    )(*ins)


def rounds():
    first, second = [], []

    def device(z, h, core, chip):
        return ((z * H + h) * N_BLK) + chip * C + core

    for chip in range(N_BLK // C):
        for h in range(H):
            first.append([device(z, h, 1, chip) for z in range(Z)])
            for q in range(2):
                second.append([device(z, h, 0, chip) for z in range(q, Z, 2)])
        for z in range(Z):
            second.append([device(z, h, 1, chip) for h in range(H)])
        for z in range(0, Z, 2):
            first.append([device(z + q, h, 0, chip) for h in range(H) for q in range(2)])
    return first, second


def exchange(value, groups):
    return lax.all_to_all(
        value, (*BULK, *BLK), 0, 0, axis_index_groups=groups, tiled=True
    )


def total(parts):
    first, second = rounds()
    got = exchange(parts.astype(jnp.float16), first)
    spread = 1.0 + lax.broadcasted_iota(jnp.float32, (FIRST, 1, 1), 0) / FIRST
    power = got[:, SLAB : SLAB + 1, HALF : HALF + 1].astype(jnp.float32)
    got = (got.astype(jnp.float32) * (jnp.exp2(power - TOP) / spread)).sum(0)
    return exchange(got.reshape(SECOND, SLOTS * SLAB, W), second).sum(0)


def local(aux_factors, tile_cols):
    row = jnp.pad(
        tile_cols.astype(jnp.bfloat16),
        ((0, 15), (0, W - SLOTS)),
        constant_values=-2,
    )
    a = aux_factors.reshape(K, W)
    rowed = jnp.concatenate([a, row])
    x = [fetch(part, right) for part in (a[: PARTS[0]], rowed[PARTS[0] :])]
    w = fetch(rowed, left)
    b = fetch(rowed, sib)
    v = [fetch(part, diag_via) for part in x]

    late_shape = (N_BULK, LATE * SLAB, W)
    shapes = [(N_BULK, EARLY * SLAB, W), (SLAB, W), late_shape]
    ins = (tile_cols, a, b, w, *x, v[0])
    *early, flags = call(early_kernel, shapes, 1, EARLY, *ins, n_flags=LATE)
    shapes = [(FIRST, SECOND * SLOTS * SLAB, W)]
    ins = (flags, a, b, w, x[1], v[1], *early)
    (parts,) = call(late_kernel, shapes, 1, LATE, *ins, scratch=[late_shape])
    done = total(parts)

    parts = [done]
    for role, sent in MAIL:
        sent = [t or 0 for t in sent]
        slabs = [done[t * SLAB : (t + 1) * SLAB] for t in sent]
        parts.append(hand(jnp.concatenate(slabs), role))
    count = sum(part.shape[0] for part in parts) // SLAB
    return call(
        pick_kernel,
        [(SLOTS, SLAB, W)],
        2,
        0,
        jnp.asarray(addresses()),
        tile_cols,
        *parts,
        scratch=[(count, SLAB, W)],
    )[0]


def solution(mesh):
    fine = Mesh(mesh.devices.reshape(Z, H, L, X, C), (*BULK, *BLK))
    in_specs = (P(BULK, None, BLK), P(BLK, None))
    out_specs = P(BLK, BULK, None)
    return jax.shard_map(
        local, mesh=fine, in_specs=in_specs, out_specs=out_specs, check_vma=False
    )
```
